256 devices in a mesh: lon: 32 (over x_hi, z, core), lat: 8 (over x_lo, y).
Axes of the slice: x: 4 (x_hi: 2, x_lo: 2; x = x_hi * 2 + x_lo), y: 4, z: 8, core: 2. Of those that a mesh axis runs over, the one named last changes fastest.
Arguments:
- earlier_state: float32 [4, 4, 512, 16384], P(None, None, 'lat', 'lon'), may hold values from -6 to 6
- present_state: float32 [4, 4, 512, 16384], P(None, None, 'lat', 'lon'), may hold values from -6 to 6
- scalar_wet_flags: int32 [4, 512, 16384], P(None, 'lat', 'lon'), may hold values 0 or 1
- eastside_wet_flags: int32 [4, 512, 16384], P(None, 'lat', 'lon'), may hold values 0 or 1
- northside_wet_flags: int32 [4, 512, 16384], P(None, 'lat', 'lon'), may hold values 0 or 1
Outputs:
- after: float32 [4, 4, 512, 16384], P(None, None, 'lat', 'lon')
- filtered: float32 [4, 4, 512, 16384], P(None, None, 'lat', 'lon')
The draws below stay inside these ranges and needn't reach their ends.
All inputs are finite; a program needn't handle non-finite values. No bound on the sum of `scalar_wet_flags` or of `eastside_wet_flags` or of `northside_wet_flags` on one device may be relied on, other than what follows from the above.
Results may differ from the reference program's by a relative error of at most 0.00002.
Values sent between devices are 32-bit elements; how exact they have to be, the bound alone decides.
A program may use at most 128 MiB of HBM per device.

```python
import jax
import jax.numpy as jnp
from jax import lax

VERTICAL_LAYERS = 4
WEST_EAST_SPAN = 16384
SOUTH_NORTH_SPAN = 512


def place_ends(result, own_key, least, high):
    extent = result.shape
    place = [jax.random.randint(jax.random.fold_in(own_key, axis), (), 0, extent[axis]) for axis in range(len(extent))]
    result = result.at[tuple(place)].set(least)
    longest = extent.index(max(extent))
    place[longest] = (place[longest] + 1) % extent[longest]
    return result.at[tuple(place)].set(high)


def steps_of(rng, shape, shards, smallest, largest):
    level = 1.0
    for dim, blocks in shards:
        draws = jax.random.uniform(jax.random.fold_in(jax.random.fold_in(rng, 6), dim), (blocks,), jnp.float32, smallest / len(shards), largest / len(shards))
        level = level * jnp.repeat(jnp.exp(draws), shape[dim] // blocks).reshape((-1,) + (1,) * (len(shape) - 1 - dim))
    return level


def gaussian(own_key, dims, scale, reach, split=(), kind=jnp.bfloat16):
    drawn = scale * jax.random.normal(own_key, dims, jnp.float32)
    if split:
        drawn = drawn * steps_of(own_key, dims, split, -0.22, 0.18)
    return jnp.clip(drawn, -reach, reach).astype(kind)


def setup_inputs(seed: int = 0) -> dict:
    streams_of = jax.random.split(jax.random.key(seed), 6)
    earlier_state = gaussian(streams_of[0], (4, VERTICAL_LAYERS, SOUTH_NORTH_SPAN, WEST_EAST_SPAN), 1.0, 6.0, ((2, 8), (3, 32)), jnp.float32)
    present_state = gaussian(streams_of[1], (4, VERTICAL_LAYERS, SOUTH_NORTH_SPAN, WEST_EAST_SPAN), 1.0, 6.0, ((2, 8), (3, 32)), jnp.float32)
    scalar_wet_flags = place_ends((jax.random.randint(streams_of[2], (VERTICAL_LAYERS, SOUTH_NORTH_SPAN, WEST_EAST_SPAN), 0, 5) < 4).astype(jnp.int32), jax.random.fold_in(streams_of[2], 1), 0, 1)
    eastside_wet_flags = place_ends((jax.random.randint(streams_of[3], (VERTICAL_LAYERS, SOUTH_NORTH_SPAN, WEST_EAST_SPAN), 0, 5) < 4).astype(jnp.int32), jax.random.fold_in(streams_of[3], 1), 0, 1)
    northside_wet_flags = place_ends((jax.random.randint(streams_of[4], (VERTICAL_LAYERS, SOUTH_NORTH_SPAN, WEST_EAST_SPAN), 0, 5) < 4).astype(jnp.int32), jax.random.fold_in(streams_of[4], 1), 0, 1)
    return {"earlier_state": earlier_state, "present_state": present_state, "scalar_wet_flags": scalar_wet_flags, "eastside_wet_flags": eastside_wet_flags, "northside_wet_flags": northside_wet_flags}


advect_coef = 0.5
diffuse_coef = 0.25
twice_step = 0.5
gravity = 0.5
coriolis = 0.5
thermal = 0.2
haline = 0.15
asselin = 0.1


def pressure(temp, salt):
    density = haline * salt - thermal * temp
    return jnp.cumsum(density, axis=0) - 0.5 * density


def face_flux(here, ahead, speed, face_mask):
    return advect_coef * speed * (here[:4] + ahead[:4]) * 0.5 - diffuse_coef * face_mask * (ahead[4:] - here[4:])


def level_step(items):
    prior, current, tracer_cell_mask, mask_u, southnorth_wet_flags, pres = items
    fmask = jnp.stack([tracer_cell_mask, tracer_cell_mask, mask_u, southnorth_wet_flags])
    curm = current * fmask
    befm = prior * fmask
    both = jnp.concatenate([curm, befm], 0)
    signs = jnp.array([1.0, 1.0, -1.0, -1.0, 1.0, 1.0, -1.0, -1.0], jnp.float32)[:, None]
    ghost = both[:, -1, ::-1] * signs
    east = jnp.roll(both, -1, -1)
    north = jnp.concatenate([both[:, 1:, :], ghost[:, None, :]], 1)
    flux_e = face_flux(both, east, curm[2], mask_u)
    northern_face_flux = face_flux(both, north, curm[3], southnorth_wet_flags)
    flux_w = jnp.roll(flux_e, 1, -1)
    flux_s = jnp.concatenate([jnp.zeros_like(northern_face_flux[:, :1, :]), northern_face_flux[:, :-1, :]], 1)
    pres_e = jnp.roll(pres, -1, -1)
    pres_n = jnp.concatenate([pres[1:, :], pres[-1:, ::-1]], 0)
    rows = jnp.arange(SOUTH_NORTH_SPAN, dtype=jnp.float32)
    cor = (coriolis * (2.0 * (rows + 0.5) / SOUTH_NORTH_SPAN - 1.0))[:, None]
    tend = -((flux_e - flux_w) + (northern_face_flux - flux_s))
    zonal_velocity_tendency = tend[2] + (cor * curm[3] - gravity * mask_u * (pres_e - pres))
    tend_v = tend[3] - (cor * curm[2] + gravity * southnorth_wet_flags * (pres_n - pres))
    tend = jnp.stack([tend[0], tend[1], zonal_velocity_tendency, tend_v])
    after = (befm + twice_step * tend) * fmask
    filtered = curm + asselin * (befm - 2.0 * curm + after)
    return after, filtered


def reference(earlier_state, present_state, scalar_wet_flags, eastside_wet_flags, northside_wet_flags):
    tracer_cell_mask = scalar_wet_flags.astype(jnp.float32)
    mask_u = eastside_wet_flags.astype(jnp.float32)
    southnorth_wet_flags = northside_wet_flags.astype(jnp.float32)
    pres = pressure(present_state[0] * tracer_cell_mask, present_state[1] * tracer_cell_mask)
    after, filtered = lax.map(level_step, (jnp.moveaxis(earlier_state, 1, 0), jnp.moveaxis(present_state, 1, 0), tracer_cell_mask, mask_u, southnorth_wet_flags, pres))
    return jnp.moveaxis(after, 0, 1), jnp.moveaxis(filtered, 0, 1)
```

```python
import functools

import jax
import jax.numpy as jnp
from jax import lax
from jax.experimental import pallas as pl
from jax.experimental.pallas import tpu as pltpu
from jax.sharding import PartitionSpec as P

advect_coef = 0.5
diffuse_coef = 0.25
twice_step = 0.5
gravity = 0.5
coriolis = 0.5
thermal = 0.2
haline = 0.15
asselin = 0.1

LANES = 128
SUB = 8
MESH = pl.DeviceIdType.MESH


def kernel(
    n_lon,
    n_lat,
    bef_hbm,
    cur_hbm,
    tm_hbm,
    um_hbm,
    vm_hbm,
    after_ref,
    filt_ref,
    st,
    mk,
    pr,
    fn,
    send_w,
    send_e,
    from_e,
    from_w,
    pres_e,
    fold,
    load_sems,
    send_sems,
    recv_sems,
):
    levels, rows, cols = tm_hbm.shape
    chunks = cols // LANES
    strips = rows // SUB
    lon, lat = lax.axis_index("lon"), lax.axis_index("lat")
    east, west = lax.rem(lon + 1, n_lon), lax.rem(lon + n_lon - 1, n_lon)
    partner = n_lon - 1 - lon
    has_north, has_south = lat < n_lat - 1, lat > 0
    is_top = lat == n_lat - 1

    barrier = pltpu.get_barrier_semaphore()
    pl.semaphore_signal(barrier, inc=1, device_id={"lon": east}, device_id_type=MESH)
    pl.semaphore_signal(barrier, inc=1, device_id={"lon": west}, device_id_type=MESH)

    @pl.when(has_north)
    def _():
        pl.semaphore_signal(barrier, inc=1, device_id={"lat": lat + 1}, device_id_type=MESH)

    @pl.when(has_south)
    def _():
        pl.semaphore_signal(barrier, inc=1, device_id={"lat": lat - 1}, device_id_type=MESH)

    @pl.when(is_top)
    def _():
        pl.semaphore_signal(barrier, inc=1, device_id={"lon": partner}, device_id_type=MESH)

    loads = []
    for i, t in enumerate(range(chunks)):
        lanes = pl.ds(LANES * t, LANES)
        inside = pl.ds(SUB, rows)
        for j, (src, dst) in enumerate(
            [
                (cur_hbm.at[:, :, :, lanes], st.at[t, 0:4, :, inside, :]),
                (bef_hbm.at[:, :, :, lanes], st.at[t, 4:8, :, inside, :]),
                (tm_hbm.at[:, :, lanes], mk.at[t, 0]),
                (um_hbm.at[:, :, lanes], mk.at[t, 1]),
                (vm_hbm.at[:, :, lanes], mk.at[t, 2]),
            ]
        ):
            copy = pltpu.make_async_copy(src, dst, load_sems.at[t, j])
            copy.start()
            loads.append(copy)
    for copy in loads:
        copy.wait()

    lane = lax.broadcasted_iota(jnp.int32, (SUB, LANES), 1)

    def mask_strip(r, carry):
        strip = pl.ds(pl.multiple_of(SUB + SUB * r, SUB), SUB)
        plain = pl.ds(pl.multiple_of(SUB * r, SUB), SUB)
        pack_w = jnp.zeros((SUB, LANES), jnp.float32)
        pack_e = jnp.zeros((SUB, LANES), jnp.float32)
        for t in range(chunks):
            total = None
            for l in range(levels):
                m = [mk[t, i, l, plain, :].astype(jnp.float32) for i in range(3)]
                fm = [m[0], m[0], m[1], m[2]]
                x = [None] * 8
                for f in range(8):
                    x[f] = st[t, f, l, strip, :] * fm[f % 4]
                    st[t, f, l, strip, :] = x[f]
                    c = f * levels + l
                    if t == 0:
                        moved = x[f] if c == 0 else pltpu.roll(x[f], c, 1)
                        pack_w = jnp.where(lane == c, moved, pack_w)
                    if t == chunks - 1:
                        pack_e = jnp.where(lane == c, pltpu.roll(x[f], c + 1, 1), pack_e)
                if t == chunks - 1:
                    c = 8 * levels + l
                    pack_e = jnp.where(lane == c, pltpu.roll(m[1], c + 1, 1), pack_e)
                rho = haline * x[1] - thermal * x[0]
                total = rho if total is None else total + rho
                pr[t, l, strip, :] = total - 0.5 * rho
                st[t, 8, l, strip, :] = m[2]
        send_w[plain, :] = pack_w
        send_e[plain, :] = pack_e
        return carry

    lax.fori_loop(0, strips, mask_strip, 0)

    @pl.when(has_south)
    def _():
        pl.semaphore_wait(barrier, 4)

    @pl.when(lat == 0)
    def _():
        pl.semaphore_wait(barrier, 3)

    def remote(src, dst, which, device):
        return pltpu.make_async_remote_copy(
            src_ref=src,
            dst_ref=dst,
            send_sem=send_sems.at[which],
            recv_sem=recv_sems.at[which],
            device_id=device,
            device_id_type=MESH,
        )

    to_west = remote(send_w, from_e, 0, {"lon": west})
    to_east = remote(send_e, from_w, 1, {"lon": east})
    to_north = remote(
        st.at[:, :, :, pl.ds(rows + SUB - 1, 1), :],
        st.at[:, :, :, pl.ds(SUB - 1, 1), :],
        2,
        {"lat": lat + 1},
    )
    to_south = remote(
        st.at[:, 0:8, :, pl.ds(SUB, 1), :],
        st.at[:, 0:8, :, pl.ds(rows + SUB, 1), :],
        3,
        {"lat": lat - 1},
    )
    to_fold = remote(st.at[:, 0:8, :, rows + SUB - 1, :], fold, 4, {"lon": partner})

    @pl.when(is_top)
    def _():
        to_fold.start()

    to_west.start()
    to_east.start()

    @pl.when(has_north)
    def _():
        to_north.start()

    @pl.when(has_south)
    def _():
        to_south.start()

    @pl.when(lat == 0)
    def _():
        for t in range(chunks):
            for f in range(9):
                for l in range(levels):
                    st[t, f, l, 0:SUB, :] = jnp.zeros((SUB, LANES), jnp.float32)

    @pl.when(has_south)
    def _():
        to_north.wait_recv()

    @pl.when(has_north)
    def _():
        to_south.wait_recv()

    @pl.when(is_top)
    def _():
        to_fold.wait_recv()
        back = LANES - 1 - lax.broadcasted_iota(jnp.int32, (levels, LANES), 1)
        for t in range(chunks):
            for f in range(8):
                y = jnp.take_along_axis(
                    fold[chunks - 1 - t, f], back, axis=1, mode="promise_in_bounds"
                )
                if f % 4 >= 2:
                    y = -y
                for l in range(levels):
                    st[t, f, l, rows + SUB : rows + SUB + 1, :] = y[l : l + 1, :]

    to_west.wait_recv()
    to_east.wait_recv()

    def face(scaled_speed, scaled_mask, h, a):
        return [
            scaled_speed * (h[k] + a[k]) - scaled_mask * (a[4 + k] - h[4 + k]) for k in range(4)
        ]

    advect = advect_coef * 0.5 * twice_step
    diffuse = diffuse_coef * twice_step

    for t in range(chunks):
        total = None
        for l in range(levels):
            h = [st[t, f, l, 0:SUB, :] for f in range(8)]
            a = [st[t, f, l, 1 : SUB + 1, :] for f in range(8)]
            flux = face(advect * h[3], diffuse * st[t, 8, l, 0:SUB, :], h, a)
            for k in range(4):
                fn[t, k, l, 0:SUB, :] = flux[k]
            edge = slice(rows + SUB, rows + 2 * SUB)
            rho = haline * st[t, 1, l, edge, :] - thermal * st[t, 0, l, edge, :]
            total = rho if total is None else total + rho
            pr[t, l, edge, :] = total - 0.5 * rho

    def east_pressure(r, carry):
        plain = pl.ds(pl.multiple_of(SUB * r, SUB), SUB)
        x = from_e[plain, :]
        rho = haline * pltpu.roll(x, LANES - levels, 1) - thermal * x
        total = rho
        for l in range(1, levels):
            total = total + jnp.where(lane >= l, pltpu.roll(rho, l, 1), 0.0)
        pres_e[plain, :] = total - 0.5 * rho
        return carry

    lax.fori_loop(0, strips, east_pressure, 0)

    def step_strip(r, carry):
        at = pl.multiple_of(SUB + SUB * r, SUB)
        plain = pl.ds(pl.multiple_of(SUB * r, SUB), SUB)
        strip, above, below = pl.ds(at, SUB), pl.ds(at + 1, SUB), pl.ds(at - 1, SUB)
        row = lat * rows + r * SUB + lax.broadcasted_iota(jnp.int32, (SUB, LANES), 0)
        cor = coriolis * (2.0 * (row.astype(jnp.float32) + 0.5) / (rows * n_lat) - 1.0)
        cor = twice_step * cor
        edge_e, edge_w, edge_p = from_e[plain, :], from_w[plain, :], pres_e[plain, :]
        first, last = lane == 0, lane == LANES - 1

        def at_last(x, c):
            return pltpu.roll(x, LANES - 1 - c, 1)

        def at_first(x, c):
            return x if c == 0 else pltpu.roll(x, LANES - c, 1)

        for l in range(levels):
            h = [st[0, f, l, strip, :] for f in range(8)]
            p = pr[0, l, strip, :]
            back = [pltpu.roll(x, LANES - 1, 1) for x in h + [p]]
            w = [at_first(edge_w, f * levels + l) for f in range(8)]
            w_mask = at_first(edge_w, 8 * levels + l)
            prior = face(advect * w[2], diffuse * w_mask, w, h)
            for t in range(chunks):
                lanes = pl.ds(LANES * t, LANES)
                if t + 1 < chunks:
                    h_next = [st[t + 1, f, l, strip, :] for f in range(8)]
                    p_next = pr[t + 1, l, strip, :]
                    back_next = [pltpu.roll(x, LANES - 1, 1) for x in h_next + [p_next]]
                else:
                    h_next = p_next = None
                    back_next = [at_last(edge_e, f * levels + l) for f in range(8)]
                    back_next.append(at_last(edge_p, l))
                a = [jnp.where(last, y, x) for x, y in zip(back, back_next)]
                m = [mk[t, i, l, plain, :].astype(jnp.float32) for i in range(3)]
                fm = [m[0], m[0], m[1], m[2]]
                flux_e = face(advect * h[2], diffuse * m[1], h, a)
                moved = [pltpu.roll(x, 1, 1) for x in flux_e]
                flux_w = [jnp.where(first, y, x) for x, y in zip(moved, prior)]
                prior = moved
                n = [st[t, f, l, above, :] for f in range(8)]
                flux_n = face(advect * h[3], diffuse * m[2], h, n)
                for k in range(4):
                    fn[t, k, l, strip, :] = flux_n[k]
                tend = [
                    (flux_w[k] - flux_e[k]) + (fn[t, k, l, below, :] - flux_n[k]) for k in range(4)
                ]
                push = gravity * twice_step
                tend[2] = tend[2] + (cor * h[3] - push * m[1] * (a[8] - p))
                tend[3] = tend[3] - (cor * h[2] + push * m[2] * (pr[t, l, above, :] - p))
                for k in range(4):
                    after = (h[4 + k] + tend[k]) * fm[k]
                    after_ref[k, l, plain, lanes] = after
                    filt_ref[k, l, plain, lanes] = (1.0 - 2.0 * asselin) * h[k] + asselin * (
                        h[4 + k] + after
                    )
                h, p, back = h_next, p_next, back_next
        return carry

    lax.fori_loop(0, strips, step_strip, 0)

    to_west.wait_send()
    to_east.wait_send()

    @pl.when(has_north)
    def _():
        to_north.wait_send()

    @pl.when(has_south)
    def _():
        to_south.wait_send()

    @pl.when(is_top)
    def _():
        to_fold.wait_send()


def shards(n_lon, n_lat, *args):
    _, levels, rows, cols = args[0].shape
    chunks = cols // LANES
    f32 = jnp.float32
    out = jax.ShapeDtypeStruct(args[0].shape, f32)
    args = [pltpu.with_memory_space_constraint(x, pltpu.HBM) for x in args]
    return pl.pallas_call(
        functools.partial(kernel, n_lon, n_lat),
        out_shape=(out, out),
        in_specs=[pl.BlockSpec(memory_space=pl.ANY)] * 5,
        out_specs=(pl.BlockSpec(memory_space=pltpu.VMEM),) * 2,
        scratch_shapes=[
            pltpu.VMEM((chunks, 9, levels, rows + 2 * SUB, LANES), f32),
            pltpu.VMEM((chunks, 3, levels, rows, LANES), jnp.int32),
            pltpu.VMEM((chunks, levels, rows + 2 * SUB, LANES), f32),
            pltpu.VMEM((chunks, 4, levels, rows + 2 * SUB, LANES), f32),
            pltpu.VMEM((rows, LANES), f32),
            pltpu.VMEM((rows, LANES), f32),
            pltpu.VMEM((rows, LANES), f32),
            pltpu.VMEM((rows, LANES), f32),
            pltpu.VMEM((rows, LANES), f32),
            pltpu.VMEM((chunks, 8, levels, LANES), f32),
            pltpu.SemaphoreType.DMA((chunks, 5)),
            pltpu.SemaphoreType.DMA((5,)),
            pltpu.SemaphoreType.DMA((5,)),
        ],
        compiler_params=pltpu.CompilerParams(
            collective_id=0, has_side_effects=True, vmem_limit_bytes=28 << 20
        ),
    )(*args)


def solution(mesh):
    state = P(None, None, "lat", "lon")
    flags = P(None, "lat", "lon")
    return jax.shard_map(
        functools.partial(shards, mesh.shape["lon"], mesh.shape["lat"]),
        mesh=mesh,
        in_specs=(state, state, flags, flags, flags),
        out_specs=(state, state),
        check_vma=False,
    )
```

```python
import functools

import jax
import jax.numpy as jnp
from jax import lax
from jax.experimental import pallas as pl
from jax.experimental.pallas import tpu as pltpu
from jax.sharding import PartitionSpec as P

advect_coef = 0.5
diffuse_coef = 0.25
twice_step = 0.5
gravity = 0.5
coriolis = 0.5
thermal = 0.2
haline = 0.15
asselin = 0.1

LANES = 128
SUB = 8
MESH = pl.DeviceIdType.MESH
DRY = 1e30


def kernel(
    n_lon,
    n_lat,
    bef_hbm,
    cur_hbm,
    tm_hbm,
    um_hbm,
    vm_hbm,
    after_ref,
    filt_ref,
    st,
    mk,
    pr,
    fn,
    own,
    from_e,
    from_w,
    top,
    bottom,
    from_n,
    from_s,
    load_sems,
    send_sems,
    recv_sems,
):
    levels, rows, cols = tm_hbm.shape
    chunks = cols // LANES
    strips = rows // SUB
    middle = range(1, chunks - 1)
    ends = sorted({0, chunks - 1})
    lon, lat = lax.axis_index("lon"), lax.axis_index("lat")
    east, west = lax.rem(lon + 1, n_lon), lax.rem(lon + n_lon - 1, n_lon)
    partner = n_lon - 1 - lon
    has_north, has_south = lat < n_lat - 1, lat > 0
    is_top = lat == n_lat - 1

    barrier = pltpu.get_barrier_semaphore()
    pl.semaphore_signal(barrier, inc=1, device_id={"lon": east}, device_id_type=MESH)
    pl.semaphore_signal(barrier, inc=1, device_id={"lon": west}, device_id_type=MESH)

    @pl.when(has_north)
    def _():
        pl.semaphore_signal(barrier, inc=1, device_id={"lat": lat + 1}, device_id_type=MESH)

    @pl.when(has_south)
    def _():
        pl.semaphore_signal(barrier, inc=1, device_id={"lat": lat - 1}, device_id_type=MESH)

    @pl.when(is_top)
    def _():
        pl.semaphore_signal(barrier, inc=1, device_id={"lon": partner}, device_id_type=MESH)

    def load(t, first, count, sem):
        lanes = pl.ds(LANES * t, LANES)
        part = pl.ds(first, count)
        copies = []
        for j, (src, dst) in enumerate(
            [
                (cur_hbm.at[:, :, part, lanes], st.at[t, 0:4, :, part, :]),
                (bef_hbm.at[:, :, part, lanes], st.at[t, 4:8, :, part, :]),
                (tm_hbm.at[:, part, lanes], mk.at[t, 0, :, part, :]),
                (um_hbm.at[:, part, lanes], mk.at[t, 1, :, part, :]),
                (vm_hbm.at[:, part, lanes], mk.at[t, 2, :, part, :]),
            ]
        ):
            copy = pltpu.make_async_copy(src, dst, load_sems.at[sem, t, j])
            copy.start()
            copies.append(copy)
        return copies

    early, late = [], []
    for t in ends:
        early += load(t, 0, rows, 0)
    for t in middle:
        early += load(t, rows - SUB, SUB, 1)
    for t in middle:
        late += load(t, 0, rows - SUB, 0)
    for copy in early:
        copy.wait()

    lane = lax.broadcasted_iota(jnp.int32, (SUB, LANES), 1)
    first, last = lane == 0, lane == LANES - 1
    nothing = jnp.zeros((SUB, LANES), jnp.float32)

    def masked(t, l, strip, total):
        m = [mk[t, i, l, strip, :].astype(jnp.float32) for i in range(3)]
        fm = [m[0], m[0], m[1], m[2]]
        x = [st[t, f, l, strip, :] * fm[f % 4] for f in range(8)]
        for f in range(8):
            st[t, f, l, strip, :] = x[f]
        rho = haline * x[1] - thermal * x[0]
        total = rho if total is None else total + rho
        pr[t, l, strip, :] = total - 0.5 * rho
        return x, m, total

    def strip_of(r):
        return pl.ds(pl.multiple_of(SUB * r, SUB), SUB)

    def outer_strip(r, packs):
        strip = strip_of(r)
        packs = list(packs)
        totals = {t: None for t in ends}
        for l in range(levels):
            values = {}
            for t in ends:
                x, m, totals[t] = masked(t, l, strip, totals[t])
                values[t] = x + [m[1], m[0], m[2]]
            shift = 2 * (r * levels + l)
            here = ((lane - shift + 1) & (LANES - 1)) < 2
            for f in range(11):
                both = jnp.where(lane < LANES // 2, values[0][f], values[chunks - 1][f])
                packs[f] = jnp.where(here, pltpu.roll(both, shift, 1), packs[f])
        return tuple(packs)

    packs = lax.fori_loop(0, strips, outer_strip, (nothing,) * 11)
    for f in range(11):
        own[f] = packs[f]

    def middle_strip(strip):
        for t in middle:
            total = None
            for l in range(levels):
                total = masked(t, l, strip, total)[2]

    def edge_row(to, row):
        for t in range(chunks):
            for l in range(levels):
                for f in range(8):
                    to[t, f, l : l + 1, :] = st[t, f, l, row : row + 1, :]
                for f, i in ((8, 2), (9, 0), (10, 1)):
                    mask = mk[t, i, l, row : row + 1, :].astype(jnp.float32)
                    to[t, f, l : l + 1, :] = mask

    middle_strip(slice(rows - SUB, rows))
    edge_row(top, rows - 1)

    @pl.when(has_south)
    def _():
        pl.semaphore_wait(barrier, 4)

    @pl.when(lat == 0)
    def _():
        pl.semaphore_wait(barrier, 3)

    def remote(src, dst, which, device):
        return pltpu.make_async_remote_copy(
            src_ref=src,
            dst_ref=dst,
            send_sem=send_sems.at[which],
            recv_sem=recv_sems.at[which],
            device_id=device,
            device_id_type=MESH,
        )

    to_west = remote(own.at[0:9], from_e, 0, {"lon": west})
    to_east = remote(own.at[0:9], from_w, 1, {"lon": east})
    to_north = remote(top.at[:, 0:9], from_s, 2, {"lat": lat + 1})
    to_south = remote(bottom.at[:, 0:8], from_n, 3, {"lat": lat - 1})
    to_fold = remote(top.at[:, 0:8], from_n, 4, {"lon": partner})

    @pl.when(is_top)
    def _():
        to_fold.start()

    to_west.start()
    to_east.start()

    @pl.when(has_north)
    def _():
        to_north.start()

    for copy in late:
        copy.wait()

    def middle_step(r, carry):
        middle_strip(strip_of(r))
        return carry

    lax.fori_loop(0, strips - 1, middle_step, 0)
    edge_row(bottom, 0)

    @pl.when(has_south)
    def _():
        to_south.start()

    for t in range(chunks):
        for l in range(levels):
            for f in range(8):
                st[t, f, l, rows : rows + SUB, :] = nothing
            for k in range(4):
                fn[t, k, l, 0:SUB, :] = nothing
            pr[t, l, rows : rows + SUB, :] = nothing

    advect = advect_coef * 0.5 * twice_step
    diffuse = diffuse_coef * twice_step
    push = gravity * twice_step
    keep = 1.0 - 2.0 * asselin

    def step_strip(r, carry):
        at = pl.multiple_of(SUB * r, SUB)
        strip, above = pl.ds(at, SUB), pl.ds(at + 1, SUB)
        put, below = pl.ds(at + SUB, SUB), pl.ds(at + SUB - 1, SUB)
        row = lat * rows + r * SUB + lax.broadcasted_iota(jnp.int32, (SUB, LANES), 0)
        cor = coriolis * (2.0 * (row.astype(jnp.float32) + 0.5) / (rows * n_lat) - 1.0)
        cor = twice_step * cor

        def finish(l, t, west_flux, east_flux):
            lanes = pl.ds(LANES * t, LANES)
            h = [st[t, f, l, strip, :] for f in range(8)]
            n = [st[t, f, l, above, :] for f in range(8)]
            m = [mk[t, i, l, strip, :].astype(jnp.float32) for i in range(3)]
            fm = [m[0], m[0], m[1], m[2]]
            p = pr[t, l, strip, :]
            speed, mask = advect * h[3], diffuse * m[2]
            tend = []
            for k in range(4):
                flux_n = speed * (h[k] + n[k]) - mask * (n[4 + k] - h[4 + k])
                fn[t, k, l, put, :] = flux_n
                tend.append((west_flux[k] - east_flux[k]) + (fn[t, k, l, below, :] - flux_n))
            tend[2] = tend[2] + (cor * h[3] + push * m[1] * p)
            tend[3] = tend[3] - (cor * h[2] + push * m[2] * (pr[t, l, above, :] - p))
            for k in range(4):
                after = (h[4 + k] + tend[k]) * fm[k]
                after_ref[k, l, strip, lanes] = after
                filt_ref[k, l, strip, lanes] = keep * h[k] + asselin * (h[4 + k] + after)

        for l in range(levels):
            prior_speed = jnp.full((SUB, LANES), DRY, jnp.float32)
            prior_part = [nothing] * 4
            waiting = None
            for t in range(chunks):
                h = [st[t, f, l, strip, :] for f in range(8)]
                wet = mk[t, 1, l, strip, :]
                speed, mask = advect * h[2], diffuse * wet.astype(jnp.float32)
                moved = pltpu.roll(jnp.where(wet > 0, h[2], DRY), 1, 1)
                speed_w = jnp.where(first, prior_speed, moved)
                prior_speed = moved
                dry = speed_w > 0.5 * DRY
                speed_w = jnp.where(dry, 0.0, advect * speed_w)
                mask_w = jnp.where(dry, 0.0, diffuse)
                flux_w, back = [], []
                for k in range(4):
                    part = pltpu.roll(speed * h[k] + mask * h[4 + k], 1, 1)
                    flux = jnp.where(first, prior_part[k], part)
                    prior_part[k] = part
                    flux = flux + (speed_w * h[k] - mask_w * h[4 + k])
                    if t == 0:
                        flux = jnp.where(first, 0.0, flux)
                    flux_w.append(flux)
                    carried = flux
                    if k == 2:
                        carried = flux + (push / diffuse) * mask_w * pr[t, l, strip, :]
                    back.append(pltpu.roll(carried, LANES - 1, 1))
                if waiting is not None:
                    flux_e = [jnp.where(last, y, x) for x, y in zip(waiting[1], back)]
                    finish(l, t - 1, waiting[0], flux_e)
                waiting = flux_w, back
            flux_e = [jnp.where(last, 0.0, x) for x in waiting[1]]
            finish(l, chunks - 1, waiting[0], flux_e)
        return carry

    lax.fori_loop(0, strips, step_strip, 0)

    def add_row(to_row, t, k, change):
        lanes = pl.ds(LANES * t, LANES)
        for l in range(levels):
            one = change[l : l + 1, :]
            after_ref[k, l, to_row : to_row + 1, lanes] += one
            filt_ref[k, l, to_row : to_row + 1, lanes] += asselin * one

    @pl.when(has_south)
    def _():
        to_north.wait_recv()
        for t in range(chunks):
            h = [from_s[t, f] for f in range(9)]
            a = [bottom[t, f] for f in range(11)]
            fm = [a[9], a[9], a[10], a[8]]
            speed, mask = advect * h[3], diffuse * h[8]
            for k in range(4):
                flux = speed * (h[k] + a[k]) - mask * (a[4 + k] - h[4 + k])
                add_row(0, t, k, flux * fm[k])

    to_west.wait_recv()
    to_east.wait_recv()

    even = (lane & 1) == 0
    left = [jnp.where(even, pltpu.roll(from_w[f], 1, 1), own[f]) for f in range(9)]
    right = [jnp.where(even, own[f], pltpu.roll(from_e[f], LANES - 1, 1)) for f in range(8)]
    rho = haline * right[1] - thermal * right[0]
    pres = 0.5 * rho
    level = (lane + 1) // 2 % levels
    for l in range(1, levels):
        pres = pres + jnp.where(level >= l, pltpu.roll(rho, 2 * l, 1), 0.0)
    speed, mask = advect * left[2], diffuse * left[8]
    fm = [own[9], own[9], own[8], own[10]]
    for k in range(4):
        flux = speed * (left[k] + right[k]) - mask * (right[4 + k] - left[4 + k])
        if k == 2:
            flux = jnp.where(even, flux, flux + push * left[8] * pres)
        from_e[k] = jnp.where(even, flux, -flux) * fm[k]

    def outer_add(r, carry):
        strip = strip_of(r)
        for k in range(4):
            change = from_e[k]
            for l in range(levels):
                one = pltpu.roll(change, LANES - 2 * (r * levels + l), 1)
                for t, where in ((0, first), (chunks - 1, last)):
                    lanes = pl.ds(LANES * t, LANES)
                    add = jnp.where(where, one, 0.0)
                    after_ref[k, l, strip, lanes] += add
                    filt_ref[k, l, strip, lanes] += asselin * add
        return carry

    lax.fori_loop(0, strips, outer_add, 0)

    @pl.when(has_north)
    def _():
        to_south.wait_recv()

    @pl.when(is_top)
    def _():
        to_fold.wait_recv()
        mirror = LANES - 1 - lax.broadcasted_iota(jnp.int32, (levels, LANES), 1)

        def turned(x):
            return jnp.take_along_axis(x, mirror, axis=1, mode="promise_in_bounds")

        for t in range((chunks + 1) // 2):
            for f in range(8):
                sign = 1.0 if f % 4 < 2 else -1.0
                a, b = from_n[t, f], from_n[chunks - 1 - t, f]
                from_n[t, f] = sign * turned(b)
                from_n[chunks - 1 - t, f] = sign * turned(a)

    for t in range(chunks):
        h = [top[t, f] for f in range(11)]
        a = [from_n[t, f] for f in range(8)]
        fm = [h[9], h[9], h[10], h[8]]
        speed, mask = advect * h[3], diffuse * h[8]
        rho = haline * a[1] - thermal * a[0]
        total, pres = None, []
        for l in range(levels):
            one = rho[l : l + 1, :]
            total = one if total is None else total + one
            pres.append(total - 0.5 * one)
        for k in range(4):
            change = mask * a[4 + k] - speed * a[k]
            if k == 3:
                change = change - push * h[8] * jnp.concatenate(pres, 0)
            add_row(rows - 1, t, k, change * fm[k])

    to_west.wait_send()
    to_east.wait_send()

    @pl.when(has_north)
    def _():
        to_north.wait_send()

    @pl.when(has_south)
    def _():
        to_south.wait_send()

    @pl.when(is_top)
    def _():
        to_fold.wait_send()


def shards(n_lon, n_lat, *args):
    _, levels, rows, cols = args[0].shape
    chunks = cols // LANES
    f32 = jnp.float32
    out = jax.ShapeDtypeStruct(args[0].shape, f32)
    args = [pltpu.with_memory_space_constraint(x, pltpu.HBM) for x in args]
    return pl.pallas_call(
        functools.partial(kernel, n_lon, n_lat),
        out_shape=(out, out),
        in_specs=[pl.BlockSpec(memory_space=pl.ANY)] * 5,
        out_specs=(pl.BlockSpec(memory_space=pltpu.VMEM),) * 2,
        scratch_shapes=[
            pltpu.VMEM((chunks, 8, levels, rows + SUB, LANES), f32),
            pltpu.VMEM((chunks, 3, levels, rows, LANES), jnp.int32),
            pltpu.VMEM((chunks, levels, rows + SUB, LANES), f32),
            pltpu.VMEM((chunks, 4, levels, rows + SUB, LANES), f32),
            pltpu.VMEM((11, SUB, LANES), f32),
            pltpu.VMEM((9, SUB, LANES), f32),
            pltpu.VMEM((9, SUB, LANES), f32),
            pltpu.VMEM((chunks, 11, levels, LANES), f32),
            pltpu.VMEM((chunks, 11, levels, LANES), f32),
            pltpu.VMEM((chunks, 8, levels, LANES), f32),
            pltpu.VMEM((chunks, 9, levels, LANES), f32),
            pltpu.SemaphoreType.DMA((2, chunks, 5)),
            pltpu.SemaphoreType.DMA((5,)),
            pltpu.SemaphoreType.DMA((5,)),
        ],
        compiler_params=pltpu.CompilerParams(
            collective_id=0, has_side_effects=True, vmem_limit_bytes=28 << 20
        ),
    )(*args)


def solution(mesh):
    state = P(None, None, "lat", "lon")
    flags = P(None, "lat", "lon")
    return jax.shard_map(
        functools.partial(shards, mesh.shape["lon"], mesh.shape["lat"]),
        mesh=mesh,
        in_specs=(state, state, flags, flags, flags),
        out_specs=(state, state),
        check_vma=False,
    )
```

```python
import functools

import jax
import jax.numpy as jnp
from jax import lax
from jax.experimental import pallas as pl
from jax.experimental.pallas import tpu as pltpu
from jax.sharding import PartitionSpec as P

advect_coef = 0.5
diffuse_coef = 0.25
twice_step = 0.5
gravity = 0.5
coriolis = 0.5
thermal = 0.2
haline = 0.15
asselin = 0.1

LANES = 128
SUB = 8
MESH = pl.DeviceIdType.MESH
DRY = 1e30
PIECES = 4


def kernel(
    n_lon,
    n_lat,
    bef_hbm,
    cur_hbm,
    tm_hbm,
    um_hbm,
    vm_hbm,
    after_ref,
    filt_ref,
    outer_ref,
    south_ref,
    north_ref,
    st,
    mk,
    pr,
    fn,
    own,
    from_e,
    from_w,
    top,
    bottom,
    from_n,
    from_s,
    load_sems,
    send_sems,
    recv_sems,
):
    levels, rows, cols = tm_hbm.shape
    chunks = cols // LANES
    strips = rows // SUB
    middle = range(1, chunks - 1)
    ends = sorted({0, chunks - 1})
    lon, lat = lax.axis_index("lon"), lax.axis_index("lat")
    east, west = lax.rem(lon + 1, n_lon), lax.rem(lon + n_lon - 1, n_lon)
    partner = n_lon - 1 - lon
    has_north, has_south = lat < n_lat - 1, lat > 0
    is_top = lat == n_lat - 1

    barrier = pltpu.get_barrier_semaphore()
    pl.semaphore_signal(barrier, inc=1, device_id={"lon": east}, device_id_type=MESH)
    pl.semaphore_signal(barrier, inc=1, device_id={"lon": west}, device_id_type=MESH)

    @pl.when(has_north)
    def _():
        pl.semaphore_signal(barrier, inc=1, device_id={"lat": lat + 1}, device_id_type=MESH)

    @pl.when(has_south)
    def _():
        pl.semaphore_signal(barrier, inc=1, device_id={"lat": lat - 1}, device_id_type=MESH)

    @pl.when(is_top)
    def _():
        pl.semaphore_signal(barrier, inc=1, device_id={"lon": partner}, device_id_type=MESH)

    def load(t, first, count, sem):
        lanes = pl.ds(LANES * t, LANES)
        part = pl.ds(first, count)
        copies = []
        for j, (src, dst) in enumerate(
            [
                (cur_hbm.at[:, :, part, lanes], st.at[t, 0:4, :, part, :]),
                (bef_hbm.at[:, :, part, lanes], st.at[t, 4:8, :, part, :]),
                (tm_hbm.at[:, part, lanes], mk.at[t, 0, :, part, :]),
                (um_hbm.at[:, part, lanes], mk.at[t, 1, :, part, :]),
                (vm_hbm.at[:, part, lanes], mk.at[t, 2, :, part, :]),
            ]
        ):
            copy = pltpu.make_async_copy(src, dst, load_sems.at[sem, t, j])
            copy.start()
            copies.append(copy)
        return copies

    piece = rows // PIECES
    highest, outer, late = [], [], []
    for t in middle:
        highest += load(t, rows - SUB, SUB, PIECES)
    for i in range(PIECES):
        outer.append([])
        for t in ends:
            outer[i] += load(t, i * piece, piece, i)
    for t in middle:
        late += load(t, 0, rows - SUB, 0)

    lane = lax.broadcasted_iota(jnp.int32, (SUB, LANES), 1)
    first, last = lane == 0, lane == LANES - 1
    nothing = jnp.zeros((SUB, LANES), jnp.float32)

    def masked(t, l, strip, total):
        m = [mk[t, i, l, strip, :].astype(jnp.float32) for i in range(3)]
        fm = [m[0], m[0], m[1], m[2]]
        x = [st[t, f, l, strip, :] * fm[f % 4] for f in range(8)]
        for f in range(8):
            st[t, f, l, strip, :] = x[f]
        rho = haline * x[1] - thermal * x[0]
        total = rho if total is None else total + rho
        pr[t, l, strip, :] = total - 0.5 * rho
        return x, m, total

    def strip_of(r):
        return pl.ds(pl.multiple_of(SUB * r, SUB), SUB)

    def outer_strip(r, packs):
        strip = strip_of(r)
        packs = list(packs)
        totals = {t: None for t in ends}
        for l in range(levels):
            values = {}
            for t in ends:
                x, m, totals[t] = masked(t, l, strip, totals[t])
                values[t] = x + [m[1]]
            shift = 2 * (r * levels + l)
            here = ((lane - shift + 1) & (LANES - 1)) < 2
            for f in range(9):
                both = jnp.where(lane < LANES // 2, values[0][f], values[chunks - 1][f])
                packs[f] = jnp.where(here, pltpu.roll(both, shift, 1), packs[f])
        return tuple(packs)

    def outer_flags(r, packs):
        strip = strip_of(r)
        packs = list(packs)
        for l in range(levels):
            shift = 2 * (r * levels + l)
            here = ((lane - shift + 1) & (LANES - 1)) < 2
            for f, i in enumerate((0, 2)):
                both = jnp.where(
                    lane < LANES // 2, mk[0, i, l, strip, :], mk[chunks - 1, i, l, strip, :]
                ).astype(jnp.float32)
                packs[f] = jnp.where(here, pltpu.roll(both, shift, 1), packs[f])
        return tuple(packs)

    def middle_strip(strip):
        for t in middle:
            total = None
            for l in range(levels):
                total = masked(t, l, strip, total)[2]

    def edge_row(to, row):
        for t in range(chunks):
            for l in range(levels):
                for f in range(8):
                    to[t, f, l : l + 1, :] = st[t, f, l, row : row + 1, :]
                for f, i in ((8, 2), (9, 0), (10, 1)):
                    mask = mk[t, i, l, row : row + 1, :].astype(jnp.float32)
                    to[t, f, l : l + 1, :] = mask

    for copy in highest:
        copy.wait()
    middle_strip(slice(rows - SUB, rows))
    packs = (nothing,) * 9
    for i in range(PIECES):
        for copy in outer[i]:
            copy.wait()
        packs = lax.fori_loop(i * piece // SUB, (i + 1) * piece // SUB, outer_strip, packs)
    for f in range(9):
        own[f] = packs[f]
    edge_row(top, rows - 1)

    @pl.when(has_south)
    def _():
        pl.semaphore_wait(barrier, 4)

    @pl.when(lat == 0)
    def _():
        pl.semaphore_wait(barrier, 3)

    def remote(src, dst, which, device):
        return pltpu.make_async_remote_copy(
            src_ref=src,
            dst_ref=dst,
            send_sem=send_sems.at[which],
            recv_sem=recv_sems.at[which],
            device_id=device,
            device_id_type=MESH,
        )

    to_west = remote(own.at[0:9], from_e, 0, {"lon": west})
    to_east = remote(own.at[0:9], from_w, 1, {"lon": east})
    to_north = remote(top.at[:, 0:9], from_s, 2, {"lat": lat + 1})
    to_south = remote(bottom.at[:, 0:8], from_n, 3, {"lat": lat - 1})
    to_fold = remote(top.at[:, 0:8], from_n, 4, {"lon": partner})

    @pl.when(is_top)
    def _():
        to_fold.start()

    to_west.start()
    to_east.start()

    @pl.when(has_north)
    def _():
        to_north.start()

    for copy in late:
        copy.wait()

    def middle_step(r, carry):
        middle_strip(strip_of(r))
        return carry

    lax.fori_loop(0, strips - 1, middle_step, 0)
    edge_row(bottom, 0)
    own[9], own[10] = lax.fori_loop(0, strips, outer_flags, (nothing,) * 2)

    @pl.when(has_south)
    def _():
        to_south.start()

    for t in range(chunks):
        for l in range(levels):
            for f in range(8):
                st[t, f, l, rows : rows + SUB, :] = nothing
            for k in range(4):
                fn[t, k, l, 0:SUB, :] = nothing
            pr[t, l, rows : rows + SUB, :] = nothing

    advect = advect_coef * 0.5 * twice_step
    diffuse = diffuse_coef * twice_step
    push = gravity * twice_step
    keep = 1.0 - 2.0 * asselin

    def step_strip(r, carry):
        at = pl.multiple_of(SUB * r, SUB)
        strip, above = pl.ds(at, SUB), pl.ds(at + 1, SUB)
        put, below = pl.ds(at + SUB, SUB), pl.ds(at + SUB - 1, SUB)
        row = lat * rows + r * SUB + lax.broadcasted_iota(jnp.int32, (SUB, LANES), 0)
        cor = coriolis * (2.0 * (row.astype(jnp.float32) + 0.5) / (rows * n_lat) - 1.0)
        cor = twice_step * cor

        def finish(l, t, west_flux, east_flux):
            lanes = pl.ds(LANES * t, LANES)
            h = [st[t, f, l, strip, :] for f in range(8)]
            n = [st[t, f, l, above, :] for f in range(8)]
            m = [mk[t, i, l, strip, :].astype(jnp.float32) for i in range(3)]
            fm = [m[0], m[0], m[1], m[2]]
            p = pr[t, l, strip, :]
            speed, mask = advect * h[3], diffuse * m[2]
            tend = []
            for k in range(4):
                flux_n = speed * (h[k] + n[k]) - mask * (n[4 + k] - h[4 + k])
                fn[t, k, l, put, :] = flux_n
                tend.append((west_flux[k] - east_flux[k]) + (fn[t, k, l, below, :] - flux_n))
            tend[2] = tend[2] + (cor * h[3] + push * m[1] * p)
            tend[3] = tend[3] - (cor * h[2] + push * m[2] * (pr[t, l, above, :] - p))
            for k in range(4):
                after = (h[4 + k] + tend[k]) * fm[k]
                after_ref[k, l, strip, lanes] = after
                filt_ref[k, l, strip, lanes] = keep * h[k] + asselin * (h[4 + k] + after)

        for l in range(levels):
            prior_speed = jnp.full((SUB, LANES), DRY, jnp.float32)
            prior_part = [nothing] * 4
            waiting = None
            for t in range(chunks):
                h = [st[t, f, l, strip, :] for f in range(8)]
                wet = mk[t, 1, l, strip, :]
                speed, mask = advect * h[2], diffuse * wet.astype(jnp.float32)
                moved = pltpu.roll(jnp.where(wet > 0, h[2], DRY), 1, 1)
                speed_w = jnp.where(first, prior_speed, moved)
                prior_speed = moved
                dry = speed_w > 0.5 * DRY
                speed_w = jnp.where(dry, 0.0, advect * speed_w)
                mask_w = jnp.where(dry, 0.0, diffuse)
                flux_w, back = [], []
                for k in range(4):
                    part = pltpu.roll(speed * h[k] + mask * h[4 + k], 1, 1)
                    flux = jnp.where(first, prior_part[k], part)
                    prior_part[k] = part
                    flux = flux + (speed_w * h[k] - mask_w * h[4 + k])
                    if t == 0:
                        flux = jnp.where(first, 0.0, flux)
                    flux_w.append(flux)
                    carried = flux
                    if k == 2:
                        carried = flux + (push / diffuse) * mask_w * pr[t, l, strip, :]
                    back.append(pltpu.roll(carried, LANES - 1, 1))
                if waiting is not None:
                    flux_e = [jnp.where(last, y, x) for x, y in zip(waiting[1], back)]
                    finish(l, t - 1, waiting[0], flux_e)
                waiting = flux_w, back
            flux_e = [jnp.where(last, 0.0, x) for x in waiting[1]]
            finish(l, chunks - 1, waiting[0], flux_e)
        return carry

    lax.fori_loop(0, strips, step_strip, 0)

    @pl.when(has_south)
    def _():
        to_north.wait_recv()
        for t in range(chunks):
            h = [from_s[t, f] for f in range(9)]
            a = [bottom[t, f] for f in range(11)]
            fm = [a[9], a[9], a[10], a[8]]
            speed, mask = advect * h[3], diffuse * h[8]
            for k in range(4):
                flux = speed * (h[k] + a[k]) - mask * (a[4 + k] - h[4 + k])
                south_ref[t, k] = flux * fm[k]

    @pl.when(lat == 0)
    def _():
        south_ref[...] = jnp.zeros(south_ref.shape, jnp.float32)

    to_west.wait_recv()
    to_east.wait_recv()

    even = (lane & 1) == 0
    left = [jnp.where(even, pltpu.roll(from_w[f], 1, 1), own[f]) for f in range(9)]
    right = [jnp.where(even, own[f], pltpu.roll(from_e[f], LANES - 1, 1)) for f in range(8)]
    rho = haline * right[1] - thermal * right[0]
    pres = 0.5 * rho
    level = (lane + 1) // 2 % levels
    for l in range(1, levels):
        pres = pres + jnp.where(level >= l, pltpu.roll(rho, 2 * l, 1), 0.0)
    speed, mask = advect * left[2], diffuse * left[8]
    fm = [own[9], own[9], own[8], own[10]]
    for k in range(4):
        flux = speed * (left[k] + right[k]) - mask * (right[4 + k] - left[4 + k])
        if k == 2:
            flux = jnp.where(even, flux, flux + push * left[8] * pres)
        outer_ref[k] = jnp.where(even, flux, -flux) * fm[k]

    @pl.when(has_north)
    def _():
        to_south.wait_recv()

    @pl.when(is_top)
    def _():
        to_fold.wait_recv()
        mirror = LANES - 1 - lax.broadcasted_iota(jnp.int32, (levels, LANES), 1)

        def turned(x):
            return jnp.take_along_axis(x, mirror, axis=1, mode="promise_in_bounds")

        for t in range((chunks + 1) // 2):
            for f in range(8):
                sign = 1.0 if f % 4 < 2 else -1.0
                a, b = from_n[t, f], from_n[chunks - 1 - t, f]
                from_n[t, f] = sign * turned(b)
                from_n[chunks - 1 - t, f] = sign * turned(a)

    for t in range(chunks):
        h = [top[t, f] for f in range(11)]
        a = [from_n[t, f] for f in range(8)]
        fm = [h[9], h[9], h[10], h[8]]
        speed, mask = advect * h[3], diffuse * h[8]
        rho = haline * a[1] - thermal * a[0]
        total, pres = None, []
        for l in range(levels):
            one = rho[l : l + 1, :]
            total = one if total is None else total + one
            pres.append(total - 0.5 * one)
        for k in range(4):
            change = mask * a[4 + k] - speed * a[k]
            if k == 3:
                change = change - push * h[8] * jnp.concatenate(pres, 0)
            north_ref[t, k] = change * fm[k]

    to_west.wait_send()
    to_east.wait_send()

    @pl.when(has_north)
    def _():
        to_north.wait_send()

    @pl.when(has_south)
    def _():
        to_south.wait_send()

    @pl.when(is_top)
    def _():
        to_fold.wait_send()


def closing_kernel(
    after_ref,
    filt_ref,
    outer_ref,
    south_ref,
    north_ref,
    after_hbm,
    filt_hbm,
    edge,
    ribbon,
    sems,
):
    _, levels, rows, cols = after_ref.shape
    chunks = cols // LANES
    strips = rows // SUB
    blocks, targets = (after_ref, filt_ref), (after_hbm, filt_hbm)
    copies = []

    def store(src, dst):
        copy = pltpu.make_async_copy(src, dst, sems.at[len(copies)])
        copy.start()
        copies.append(copy)

    inner_lanes = pl.ds(LANES, cols - 2 * LANES)
    inner_rows = pl.ds(SUB, rows - 2 * SUB)
    for src, dst in zip(blocks, targets):
        place = (slice(None), slice(None), inner_rows, inner_lanes)
        store(src.at[place], dst.at[place])

    lane = lax.broadcasted_iota(jnp.int32, (SUB, LANES), 1)
    sub = lax.broadcasted_iota(jnp.int32, (SUB, LANES), 0)
    sides = ((south_ref, 0, 0), (north_ref, rows - SUB, SUB - 1))

    def row_change(ref, t, k, l, where):
        one = jnp.broadcast_to(ref[t, k, l : l + 1, :], (SUB, LANES))
        return jnp.where(sub == where, one, 0.0)

    for i, (ref, row, where) in enumerate(sides):
        for k in range(4):
            for l in range(levels):
                for t in range(1, chunks - 1):
                    lanes = pl.ds(LANES * t, LANES)
                    change = row_change(ref, t, k, l, where)
                    to = pl.ds(LANES * (t - 1), LANES)
                    ribbon[0, i, k, l, :, to] = after_ref[k, l, row : row + SUB, lanes] + change
                    ribbon[1, i, k, l, :, to] = (
                        filt_ref[k, l, row : row + SUB, lanes] + asselin * change
                    )
        for o in range(2):
            store(ribbon.at[o, i], targets[o].at[:, :, pl.ds(row, SUB), inner_lanes])

    def outer_strip(r, carry):
        strip = pl.ds(pl.multiple_of(SUB * r, SUB), SUB)
        for k in range(4):
            for l in range(levels):
                one = pltpu.roll(outer_ref[k], LANES - 2 * (r * levels + l), 1)
                for i, (t, where) in enumerate(((0, 0), (chunks - 1, LANES - 1))):
                    lanes = pl.ds(LANES * t, LANES)
                    change = jnp.where(lane == where, one, 0.0)
                    edge[0, i, k, l, strip, :] = after_ref[k, l, strip, lanes] + change
                    edge[1, i, k, l, strip, :] = filt_ref[k, l, strip, lanes] + asselin * change
        return carry

    piece = rows // PIECES
    for part in range(PIECES):
        lax.fori_loop(part * piece // SUB, (part + 1) * piece // SUB, outer_strip, 0)
        for ref, row, where in sides:
            if part * piece <= row < (part + 1) * piece:
                for k in range(4):
                    for l in range(levels):
                        for i, t in enumerate((0, chunks - 1)):
                            change = row_change(ref, t, k, l, where)
                            edge[0, i, k, l, row : row + SUB, :] += change
                            edge[1, i, k, l, row : row + SUB, :] += asselin * change
        span = pl.ds(part * piece, piece)
        for o in range(2):
            for i, t in enumerate((0, chunks - 1)):
                store(
                    edge.at[o, i, :, :, span, :],
                    targets[o].at[:, :, span, pl.ds(LANES * t, LANES)],
                )

    for copy in copies:
        copy.wait()


def shards(n_lon, n_lat, *args):
    _, levels, rows, cols = args[0].shape
    chunks = cols // LANES
    f32 = jnp.float32
    out = jax.ShapeDtypeStruct(args[0].shape, f32)
    args = [pltpu.with_memory_space_constraint(x, pltpu.HBM) for x in args]
    block = pl.BlockSpec(memory_space=pltpu.VMEM)
    parts = pl.pallas_call(
        functools.partial(kernel, n_lon, n_lat),
        out_shape=(
            out,
            out,
            jax.ShapeDtypeStruct((4, SUB, LANES), f32),
            jax.ShapeDtypeStruct((chunks, 4, levels, LANES), f32),
            jax.ShapeDtypeStruct((chunks, 4, levels, LANES), f32),
        ),
        in_specs=[pl.BlockSpec(memory_space=pl.ANY)] * 5,
        out_specs=(block,) * 5,
        scratch_shapes=[
            pltpu.VMEM((chunks, 8, levels, rows + SUB, LANES), f32),
            pltpu.VMEM((chunks, 3, levels, rows, LANES), jnp.int32),
            pltpu.VMEM((chunks, levels, rows + SUB, LANES), f32),
            pltpu.VMEM((chunks, 4, levels, rows + SUB, LANES), f32),
            pltpu.VMEM((11, SUB, LANES), f32),
            pltpu.VMEM((9, SUB, LANES), f32),
            pltpu.VMEM((9, SUB, LANES), f32),
            pltpu.VMEM((chunks, 11, levels, LANES), f32),
            pltpu.VMEM((chunks, 11, levels, LANES), f32),
            pltpu.VMEM((chunks, 8, levels, LANES), f32),
            pltpu.VMEM((chunks, 9, levels, LANES), f32),
            pltpu.SemaphoreType.DMA((PIECES + 1, chunks, 5)),
            pltpu.SemaphoreType.DMA((5,)),
            pltpu.SemaphoreType.DMA((5,)),
        ],
        compiler_params=pltpu.CompilerParams(
            collective_id=0, has_side_effects=True, vmem_limit_bytes=28 << 20
        ),
    )(*args)
    parts = [pltpu.with_memory_space_constraint(x, pltpu.VMEM) for x in parts]
    return pl.pallas_call(
        closing_kernel,
        out_shape=(out, out),
        in_specs=[block] * 5,
        out_specs=(pl.BlockSpec(memory_space=pl.ANY),) * 2,
        scratch_shapes=[
            pltpu.VMEM((2, 2, 4, levels, rows, LANES), f32),
            pltpu.VMEM((2, 2, 4, levels, SUB, cols - 2 * LANES), f32),
            pltpu.SemaphoreType.DMA((6 + 4 * PIECES,)),
        ],
        compiler_params=pltpu.CompilerParams(vmem_limit_bytes=28 << 20),
    )(*parts)


def solution(mesh):
    state = P(None, None, "lat", "lon")
    flags = P(None, "lat", "lon")
    return jax.shard_map(
        functools.partial(shards, mesh.shape["lon"], mesh.shape["lat"]),
        mesh=mesh,
        in_specs=(state, state, flags, flags, flags),
        out_specs=(state, state),
        check_vma=False,
    )
```

```python
import functools

import jax
import jax.numpy as jnp
from jax import lax
from jax.experimental import pallas as pl
from jax.experimental.pallas import tpu as pltpu
from jax.sharding import PartitionSpec as P

advect_coef = 0.5
diffuse_coef = 0.25
twice_step = 0.5
gravity = 0.5
coriolis = 0.5
thermal = 0.2
haline = 0.15
asselin = 0.1

LANES = 128
SUB = 8
MESH = pl.DeviceIdType.MESH
DRY = 1e30
PIECES = 4


def kernel(
    n_lon,
    n_lat,
    bef_hbm,
    cur_hbm,
    tm_hbm,
    um_hbm,
    vm_hbm,
    after_ref,
    filt_ref,
    outer_ref,
    south_ref,
    north_ref,
    st,
    mk,
    pr,
    fn,
    raw,
    raw_flags,
    own_e,
    own_w,
    flags,
    from_e,
    from_w,
    top,
    bottom,
    from_n,
    from_s,
    load_sems,
    send_sems,
    recv_sems,
):
    levels, rows, cols = tm_hbm.shape
    chunks = cols // LANES
    strips = rows // SUB
    middle = range(1, chunks - 1)
    high = rows - SUB
    lon, lat = lax.axis_index("lon"), lax.axis_index("lat")
    east, west = lax.rem(lon + 1, n_lon), lax.rem(lon + n_lon - 1, n_lon)
    partner = n_lon - 1 - lon
    has_north, has_south = lat < n_lat - 1, lat > 0
    is_top = lat == n_lat - 1
    across = lax.rem(lon, n_lon // 2)
    sends_last = jnp.logical_and(is_top, across < n_lon // 4)
    sends_first = jnp.logical_not(sends_last)
    answers = across == 0
    starts = jnp.logical_not(answers)

    barrier = pltpu.get_barrier_semaphore()
    pl.semaphore_signal(barrier, inc=1, device_id={"lon": west}, device_id_type=MESH)

    @pl.when(across != n_lon // 2 - 1)
    def _():
        pl.semaphore_signal(barrier, inc=1, device_id={"lon": east}, device_id_type=MESH)

    @pl.when(has_north)
    def _():
        pl.semaphore_signal(barrier, inc=1, device_id={"lat": lat + 1}, device_id_type=MESH)

    @pl.when(has_south)
    def _():
        pl.semaphore_signal(barrier, inc=1, device_id={"lat": lat - 1}, device_id_type=MESH)

    @pl.when(is_top)
    def _():
        pl.semaphore_signal(barrier, inc=1, device_id={"lon": partner}, device_id_type=MESH)

    def load(sem, pairs):
        copies = []
        for i, (src, dst) in enumerate(pairs):
            copy = pltpu.make_async_copy(src, dst, load_sems.at[sem, i])
            copy.start()
            copies.append(copy)
        return copies

    def load_tiles(sem, t, begin, end):
        lanes = pl.ds(LANES * t, LANES)
        part = pl.ds(begin, end - begin)
        return load(
            sem,
            [
                (cur_hbm.at[:, :, part, lanes], st.at[t, 0:4, :, part, :]),
                (bef_hbm.at[:, :, part, lanes], st.at[t, 4:8, :, part, :]),
                (tm_hbm.at[:, part, lanes], mk.at[t, 0, :, part, :]),
                (um_hbm.at[:, part, lanes], mk.at[t, 1, :, part, :]),
                (vm_hbm.at[:, part, lanes], mk.at[t, 2, :, part, :]),
            ],
        )

    part = pl.ds(high, SUB)
    highest = load(
        0,
        [
            (cur_hbm.at[:, :, part, :], raw.at[0:4]),
            (bef_hbm.at[:, :, part, :], raw.at[4:8]),
            (tm_hbm.at[:, part, :], raw_flags.at[0]),
            (um_hbm.at[:, part, :], raw_flags.at[1]),
            (vm_hbm.at[:, part, :], raw_flags.at[2]),
        ],
    )
    half = strips // 2
    eastern = [
        load_tiles(1, chunks - 1, 0, SUB * half),
        load_tiles(2, chunks - 1, SUB * half, high),
    ]

    greetings = 3 + has_south.astype(jnp.int32) - answers.astype(jnp.int32)

    lane = lax.broadcasted_iota(jnp.int32, (SUB, LANES), 1)
    first, last = lane == 0, lane == LANES - 1
    nothing = jnp.zeros((SUB, LANES), jnp.float32)

    def masked(t, l, strip, total, x=None, m=None):
        if x is None:
            x = [st[t, f, l, strip, :] for f in range(8)]
            m = [mk[t, i, l, strip, :] for i in range(3)]
        m = [y.astype(jnp.float32) for y in m]
        fm = [m[0], m[0], m[1], m[2]]
        x = [x[f] * fm[f % 4] for f in range(8)]
        for f in range(8):
            st[t, f, l, strip, :] = x[f]
        rho = haline * x[1] - thermal * x[0]
        total = rho if total is None else total + rho
        pr[t, l, strip, :] = total - 0.5 * rho
        return x, m, total

    def strip_of(r):
        return pl.ds(pl.multiple_of(SUB * r, SUB), SUB)

    def pack(packs, values, shift, place):
        here = lane == ((shift + place) & (LANES - 1))
        return [
            jnp.where(here, pltpu.roll(x, shift, 1), old) for x, old in zip(values, packs)
        ]

    def eastern_strip(r, packs):
        total = None
        for l in range(levels):
            x, m, total = masked(chunks - 1, l, strip_of(r), total)
            packs = pack(packs, x + [m[1]], 2 * (r * levels + l), -1)
        return tuple(packs)

    def western_strip(r, packs):
        total = None
        for l in range(levels):
            x, m, total = masked(0, l, strip_of(r), total)
            packs = pack(packs, x, 2 * (r * levels + l), 0)
        return tuple(packs)

    def outer_flags(r, packs):
        strip = strip_of(r)
        packs = list(packs)
        for l in range(levels):
            shift = 2 * (r * levels + l)
            here = ((lane - shift + 1) & (LANES - 1)) < 2
            for i in range(3):
                both = jnp.where(
                    lane < LANES // 2, mk[0, i, l, strip, :], mk[chunks - 1, i, l, strip, :]
                ).astype(jnp.float32)
                packs[i] = jnp.where(here, pltpu.roll(both, shift, 1), packs[i])
        return tuple(packs)

    def middle_strip(strip):
        for t in middle:
            total = None
            for l in range(levels):
                total = masked(t, l, strip, total)[2]

    def edge_row(to, row):
        for t in range(chunks):
            for l in range(levels):
                for f in range(8):
                    to[t, f, l : l + 1, :] = st[t, f, l, row : row + 1, :]
                for f, i in ((8, 2), (9, 0), (10, 1)):
                    mask = mk[t, i, l, row : row + 1, :].astype(jnp.float32)
                    to[t, f, l : l + 1, :] = mask

    def remote(src, dst, which, device):
        return pltpu.make_async_remote_copy(
            src_ref=src,
            dst_ref=dst,
            send_sem=send_sems.at[which],
            recv_sem=recv_sems.at[which],
            device_id=device,
            device_id_type=MESH,
        )

    to_west = remote(own_w, from_e, 0, {"lon": west})
    to_east = remote(own_e, from_w, 1, {"lon": east})
    to_north = remote(top.at[:, 0:9], from_s, 2, {"lat": lat + 1})
    to_south = remote(bottom.at[:, 0:8], from_n, 3, {"lat": lat - 1})
    to_fold = [
        remote(top.at[t, 0:8], from_n.at[t], 4 + t, {"lon": partner}) for t in range(chunks)
    ]

    for copy in highest:
        copy.wait()
    top_strip = slice(high, rows)
    for t in range(chunks):
        lanes = slice(LANES * t, LANES * (t + 1))
        total = None
        for l in range(levels):
            m = [raw_flags[i, l, :, lanes] for i in range(3)]
            for i in range(3):
                mk[t, i, l, top_strip, :] = m[i]
            x = [raw[f, l, :, lanes] for f in range(8)]
            total = masked(t, l, top_strip, total, x, m)[2]
    edge_row(top, rows - 1)

    @pl.when(jnp.logical_and(is_top, sends_first))
    def _():
        pl.semaphore_wait(barrier, greetings)
        for copy in to_fold:
            copy.start()

    packs = [nothing] * 9
    for l in range(levels):
        x = [st[chunks - 1, f, l, top_strip, :] for f in range(8)]
        x.append(mk[chunks - 1, 1, l, top_strip, :].astype(jnp.float32))
        packs = pack(packs, x, 2 * ((strips - 1) * levels + l), -1)
    packs = tuple(packs)
    for copy in eastern[0]:
        copy.wait()
    packs = lax.fori_loop(0, half, eastern_strip, packs)
    for copy in eastern[1]:
        copy.wait()
    western = load_tiles(3, 0, 0, high)
    inner = [load_tiles(3 + t, t, 0, high) for t in middle]
    packs = lax.fori_loop(half, strips - 1, eastern_strip, packs)
    for f in range(9):
        own_e[f] = packs[f]

    @pl.when(has_north)
    def _():
        pl.semaphore_wait(barrier, greetings)

    @pl.when(sends_first)
    def _():
        to_east.start()

    @pl.when(has_north)
    def _():
        to_north.start()

    packs = [nothing] * 8
    for l in range(levels):
        x = [st[0, f, l, top_strip, :] for f in range(8)]
        packs = pack(packs, x, 2 * ((strips - 1) * levels + l), 0)
    for copy in western:
        copy.wait()
    packs = lax.fori_loop(0, strips - 1, western_strip, tuple(packs))
    for f in range(8):
        own_w[f] = packs[f]
    @pl.when(jnp.logical_and(sends_first, starts))
    def _():
        to_west.start()

    def middle_step(r, carry):
        middle_strip(strip_of(r))
        return carry

    for copies in inner:
        for copy in copies:
            copy.wait()
    lax.fori_loop(0, strips - 1, middle_step, 0)
    edge_row(bottom, 0)

    @pl.when(jnp.logical_and(sends_first, has_south))
    def _():
        to_south.start()

    packs = lax.fori_loop(0, strips, outer_flags, (nothing,) * 3)
    for i in range(3):
        flags[i] = packs[i]

    for t in range(chunks):
        for l in range(levels):
            for f in range(8):
                st[t, f, l, rows : rows + SUB, :] = nothing
            for k in range(4):
                fn[t, k, l, 0:SUB, :] = nothing
            pr[t, l, rows : rows + SUB, :] = nothing

    advect = advect_coef * 0.5 * twice_step
    diffuse = diffuse_coef * twice_step
    push = gravity * twice_step
    keep = 1.0 - 2.0 * asselin

    def step_strip(r, carry):
        at = pl.multiple_of(SUB * r, SUB)
        strip, above = pl.ds(at, SUB), pl.ds(at + 1, SUB)
        put, below = pl.ds(at + SUB, SUB), pl.ds(at + SUB - 1, SUB)
        row = lat * rows + r * SUB + lax.broadcasted_iota(jnp.int32, (SUB, LANES), 0)
        cor = coriolis * (2.0 * (row.astype(jnp.float32) + 0.5) / (rows * n_lat) - 1.0)
        cor = twice_step * cor

        def finish(l, t, west_flux, east_flux):
            lanes = pl.ds(LANES * t, LANES)
            h = [st[t, f, l, strip, :] for f in range(8)]
            n = [st[t, f, l, above, :] for f in range(8)]
            m = [mk[t, i, l, strip, :].astype(jnp.float32) for i in range(3)]
            fm = [m[0], m[0], m[1], m[2]]
            p = pr[t, l, strip, :]
            speed, mask = advect * h[3], diffuse * m[2]
            tend = []
            for k in range(4):
                flux_n = speed * (h[k] + n[k]) - mask * (n[4 + k] - h[4 + k])
                fn[t, k, l, put, :] = flux_n
                tend.append((west_flux[k] - east_flux[k]) + (fn[t, k, l, below, :] - flux_n))
            tend[2] = tend[2] + (cor * h[3] + push * m[1] * p)
            tend[3] = tend[3] - (cor * h[2] + push * m[2] * (pr[t, l, above, :] - p))
            for k in range(4):
                after = (h[4 + k] + tend[k]) * fm[k]
                after_ref[k, l, strip, lanes] = after
                filt_ref[k, l, strip, lanes] = keep * h[k] + asselin * (h[4 + k] + after)

        for l in range(levels):
            prior_speed = jnp.full((SUB, LANES), DRY, jnp.float32)
            prior_part = [nothing] * 4
            waiting = None
            for t in range(chunks):
                h = [st[t, f, l, strip, :] for f in range(8)]
                wet = mk[t, 1, l, strip, :]
                speed, mask = advect * h[2], diffuse * wet.astype(jnp.float32)
                moved = pltpu.roll(jnp.where(wet > 0, h[2], DRY), 1, 1)
                speed_w = jnp.where(first, prior_speed, moved)
                prior_speed = moved
                dry = speed_w > 0.5 * DRY
                speed_w = jnp.where(dry, 0.0, advect * speed_w)
                mask_w = jnp.where(dry, 0.0, diffuse)
                flux_w, back = [], []
                for k in range(4):
                    part = pltpu.roll(speed * h[k] + mask * h[4 + k], 1, 1)
                    flux = jnp.where(first, prior_part[k], part)
                    prior_part[k] = part
                    flux = flux + (speed_w * h[k] - mask_w * h[4 + k])
                    if t == 0:
                        flux = jnp.where(first, 0.0, flux)
                    flux_w.append(flux)
                    carried = flux
                    if k == 2:
                        carried = flux + (push / diffuse) * mask_w * pr[t, l, strip, :]
                    back.append(pltpu.roll(carried, LANES - 1, 1))
                if waiting is not None:
                    flux_e = [jnp.where(last, y, x) for x, y in zip(waiting[1], back)]
                    finish(l, t - 1, waiting[0], flux_e)
                waiting = flux_w, back
            flux_e = [jnp.where(last, 0.0, x) for x in waiting[1]]
            finish(l, chunks - 1, waiting[0], flux_e)
        return carry

    lax.fori_loop(0, strips, step_strip, 0)

    @pl.when(sends_last)
    def _():
        pl.semaphore_wait(barrier, greetings)
        for copy in to_fold:
            copy.start()
        to_south.start()
        to_east.start()

    @pl.when(jnp.logical_and(sends_last, starts))
    def _():
        to_west.start()

    @pl.when(has_south)
    def _():
        to_north.wait_recv()
        for t in range(chunks):
            h = [from_s[t, f] for f in range(9)]
            a = [bottom[t, f] for f in range(11)]
            fm = [a[9], a[9], a[10], a[8]]
            speed, mask = advect * h[3], diffuse * h[8]
            for k in range(4):
                flux = speed * (h[k] + a[k]) - mask * (a[4 + k] - h[4 + k])
                south_ref[t, k] = flux * fm[k]

    @pl.when(lat == 0)
    def _():
        south_ref[...] = jnp.zeros(south_ref.shape, jnp.float32)

    to_east.wait_recv()

    @pl.when(answers)
    def _():
        to_west.start()

    to_west.wait_recv()

    even = (lane & 1) == 0
    left = [jnp.where(even, pltpu.roll(from_w[f], 1, 1), own_e[f]) for f in range(9)]
    right = [jnp.where(even, own_w[f], pltpu.roll(from_e[f], LANES - 1, 1)) for f in range(8)]
    rho = haline * right[1] - thermal * right[0]
    pres = 0.5 * rho
    level = (lane + 1) // 2 % levels
    for l in range(1, levels):
        pres = pres + jnp.where(level >= l, pltpu.roll(rho, 2 * l, 1), 0.0)
    speed, mask = advect * left[2], diffuse * left[8]
    fm = [flags[0], flags[0], flags[1], flags[2]]
    for k in range(4):
        flux = speed * (left[k] + right[k]) - mask * (right[4 + k] - left[4 + k])
        if k == 2:
            flux = jnp.where(even, flux, flux + push * left[8] * pres)
        outer_ref[k] = jnp.where(even, flux, -flux) * fm[k]

    @pl.when(has_north)
    def _():
        to_south.wait_recv()

    @pl.when(is_top)
    def _():
        for copy in to_fold:
            copy.wait_recv()
        mirror = LANES - 1 - lax.broadcasted_iota(jnp.int32, (levels, LANES), 1)

        def turned(x):
            return jnp.take_along_axis(x, mirror, axis=1, mode="promise_in_bounds")

        for t in range((chunks + 1) // 2):
            for f in range(8):
                sign = 1.0 if f % 4 < 2 else -1.0
                a, b = from_n[t, f], from_n[chunks - 1 - t, f]
                from_n[t, f] = sign * turned(b)
                from_n[chunks - 1 - t, f] = sign * turned(a)

    for t in range(chunks):
        h = [top[t, f] for f in range(11)]
        a = [from_n[t, f] for f in range(8)]
        fm = [h[9], h[9], h[10], h[8]]
        speed, mask = advect * h[3], diffuse * h[8]
        rho = haline * a[1] - thermal * a[0]
        total, pres = None, []
        for l in range(levels):
            one = rho[l : l + 1, :]
            total = one if total is None else total + one
            pres.append(total - 0.5 * one)
        for k in range(4):
            change = mask * a[4 + k] - speed * a[k]
            if k == 3:
                change = change - push * h[8] * jnp.concatenate(pres, 0)
            north_ref[t, k] = change * fm[k]

    to_west.wait_send()
    to_east.wait_send()

    @pl.when(has_north)
    def _():
        to_north.wait_send()

    @pl.when(has_south)
    def _():
        to_south.wait_send()

    @pl.when(is_top)
    def _():
        for copy in to_fold:
            copy.wait_send()


def closing_kernel(
    after_ref,
    filt_ref,
    outer_ref,
    south_ref,
    north_ref,
    after_hbm,
    filt_hbm,
    edge,
    ribbon,
    sems,
):
    _, levels, rows, cols = after_ref.shape
    chunks = cols // LANES
    strips = rows // SUB
    blocks, targets = (after_ref, filt_ref), (after_hbm, filt_hbm)
    copies = []

    def store(src, dst):
        copy = pltpu.make_async_copy(src, dst, sems.at[len(copies)])
        copy.start()
        copies.append(copy)

    inner_lanes = pl.ds(LANES, cols - 2 * LANES)
    inner_rows = pl.ds(SUB, rows - 2 * SUB)
    for src, dst in zip(blocks, targets):
        place = (slice(None), slice(None), inner_rows, inner_lanes)
        store(src.at[place], dst.at[place])

    lane = lax.broadcasted_iota(jnp.int32, (SUB, LANES), 1)
    sub = lax.broadcasted_iota(jnp.int32, (SUB, LANES), 0)
    sides = ((south_ref, 0, 0), (north_ref, rows - SUB, SUB - 1))

    def row_change(ref, t, k, l, where):
        one = jnp.broadcast_to(ref[t, k, l : l + 1, :], (SUB, LANES))
        return jnp.where(sub == where, one, 0.0)

    for i, (ref, row, where) in enumerate(sides):
        for k in range(4):
            for l in range(levels):
                for t in range(1, chunks - 1):
                    lanes = pl.ds(LANES * t, LANES)
                    change = row_change(ref, t, k, l, where)
                    to = pl.ds(LANES * (t - 1), LANES)
                    ribbon[0, i, k, l, :, to] = after_ref[k, l, row : row + SUB, lanes] + change
                    ribbon[1, i, k, l, :, to] = (
                        filt_ref[k, l, row : row + SUB, lanes] + asselin * change
                    )
        for o in range(2):
            store(ribbon.at[o, i], targets[o].at[:, :, pl.ds(row, SUB), inner_lanes])

    def outer_strip(r, carry):
        strip = pl.ds(pl.multiple_of(SUB * r, SUB), SUB)
        for k in range(4):
            for l in range(levels):
                one = pltpu.roll(outer_ref[k], LANES - 2 * (r * levels + l), 1)
                for i, (t, where) in enumerate(((0, 0), (chunks - 1, LANES - 1))):
                    lanes = pl.ds(LANES * t, LANES)
                    change = jnp.where(lane == where, one, 0.0)
                    edge[0, i, k, l, strip, :] = after_ref[k, l, strip, lanes] + change
                    edge[1, i, k, l, strip, :] = filt_ref[k, l, strip, lanes] + asselin * change
        return carry

    piece = rows // PIECES
    for part in range(PIECES):
        lax.fori_loop(part * piece // SUB, (part + 1) * piece // SUB, outer_strip, 0)
        for ref, row, where in sides:
            if part * piece <= row < (part + 1) * piece:
                for k in range(4):
                    for l in range(levels):
                        for i, t in enumerate((0, chunks - 1)):
                            change = row_change(ref, t, k, l, where)
                            edge[0, i, k, l, row : row + SUB, :] += change
                            edge[1, i, k, l, row : row + SUB, :] += asselin * change
        span = pl.ds(part * piece, piece)
        for o in range(2):
            for i, t in enumerate((0, chunks - 1)):
                store(
                    edge.at[o, i, :, :, span, :],
                    targets[o].at[:, :, span, pl.ds(LANES * t, LANES)],
                )

    for copy in copies:
        copy.wait()


def shards(n_lon, n_lat, *args):
    _, levels, rows, cols = args[0].shape
    chunks = cols // LANES
    f32 = jnp.float32
    out = jax.ShapeDtypeStruct(args[0].shape, f32)
    args = [pltpu.with_memory_space_constraint(x, pltpu.HBM) for x in args]
    block = pl.BlockSpec(memory_space=pltpu.VMEM)
    parts = pl.pallas_call(
        functools.partial(kernel, n_lon, n_lat),
        out_shape=(
            out,
            out,
            jax.ShapeDtypeStruct((4, SUB, LANES), f32),
            jax.ShapeDtypeStruct((chunks, 4, levels, LANES), f32),
            jax.ShapeDtypeStruct((chunks, 4, levels, LANES), f32),
        ),
        in_specs=[pl.BlockSpec(memory_space=pl.ANY)] * 5,
        out_specs=(block,) * 5,
        scratch_shapes=[
            pltpu.VMEM((chunks, 8, levels, rows + SUB, LANES), f32),
            pltpu.VMEM((chunks, 3, levels, rows, LANES), jnp.int32),
            pltpu.VMEM((chunks, levels, rows + SUB, LANES), f32),
            pltpu.VMEM((chunks, 4, levels, rows + SUB, LANES), f32),
            pltpu.VMEM((8, levels, SUB, cols), f32),
            pltpu.VMEM((3, levels, SUB, cols), jnp.int32),
            pltpu.VMEM((9, SUB, LANES), f32),
            pltpu.VMEM((8, SUB, LANES), f32),
            pltpu.VMEM((3, SUB, LANES), f32),
            pltpu.VMEM((8, SUB, LANES), f32),
            pltpu.VMEM((9, SUB, LANES), f32),
            pltpu.VMEM((chunks, 11, levels, LANES), f32),
            pltpu.VMEM((chunks, 11, levels, LANES), f32),
            pltpu.VMEM((chunks, 8, levels, LANES), f32),
            pltpu.VMEM((chunks, 9, levels, LANES), f32),
            pltpu.SemaphoreType.DMA((chunks + 2, 5)),
            pltpu.SemaphoreType.DMA((4 + chunks,)),
            pltpu.SemaphoreType.DMA((4 + chunks,)),
        ],
        compiler_params=pltpu.CompilerParams(
            collective_id=0, has_side_effects=True, vmem_limit_bytes=28 << 20
        ),
    )(*args)
    parts = [pltpu.with_memory_space_constraint(x, pltpu.VMEM) for x in parts]
    return pl.pallas_call(
        closing_kernel,
        out_shape=(out, out),
        in_specs=[block] * 5,
        out_specs=(pl.BlockSpec(memory_space=pl.ANY),) * 2,
        scratch_shapes=[
            pltpu.VMEM((2, 2, 4, levels, rows, LANES), f32),
            pltpu.VMEM((2, 2, 4, levels, SUB, cols - 2 * LANES), f32),
            pltpu.SemaphoreType.DMA((6 + 4 * PIECES,)),
        ],
        compiler_params=pltpu.CompilerParams(vmem_limit_bytes=28 << 20),
    )(*parts)


def solution(mesh):
    state = P(None, None, "lat", "lon")
    flags = P(None, "lat", "lon")
    return jax.shard_map(
        functools.partial(shards, mesh.shape["lon"], mesh.shape["lat"]),
        mesh=mesh,
        in_specs=(state, state, flags, flags, flags),
        out_specs=(state, state),
        check_vma=False,
    )
```

```python
import functools

import jax
import jax.numpy as jnp
from jax import lax
from jax.experimental import pallas as pl
from jax.experimental.pallas import tpu as pltpu
from jax.sharding import PartitionSpec as P

advect_coef = 0.5
diffuse_coef = 0.25
twice_step = 0.5
gravity = 0.5
coriolis = 0.5
thermal = 0.2
haline = 0.15
asselin = 0.1

LANES = 128
SUB = 8
MESH = pl.DeviceIdType.MESH
DRY = 1e30
PIECES = 4


def kernel(
    n_lon,
    n_lat,
    bef_hbm,
    cur_hbm,
    tm_hbm,
    um_hbm,
    vm_hbm,
    after_ref,
    filt_ref,
    outer_ref,
    south_ref,
    north_ref,
    st,
    mk,
    pr,
    fn,
    raw,
    raw_flags,
    own_e,
    own_w,
    flags,
    from_e,
    from_w,
    top,
    bottom,
    from_n,
    from_s,
    load_sems,
    send_sems,
    recv_sems,
):
    levels, rows, cols = tm_hbm.shape
    chunks = cols // LANES
    strips = rows // SUB
    middle = range(1, chunks - 1)
    high = rows - SUB
    lon, lat = lax.axis_index("lon"), lax.axis_index("lat")
    east, west = lax.rem(lon + 1, n_lon), lax.rem(lon + n_lon - 1, n_lon)
    partner = n_lon - 1 - lon
    has_north, has_south = lat < n_lat - 1, lat > 0
    is_top = lat == n_lat - 1
    across = lax.rem(lon, n_lon // 2)
    sends_last = jnp.logical_and(is_top, across < 3 * n_lon // 16)
    sends_first = jnp.logical_not(sends_last)
    answers = across == 0
    starts = jnp.logical_not(answers)

    barrier = pltpu.get_barrier_semaphore()
    pl.semaphore_signal(barrier, inc=1, device_id={"lon": west}, device_id_type=MESH)

    @pl.when(across != n_lon // 2 - 1)
    def _():
        pl.semaphore_signal(barrier, inc=1, device_id={"lon": east}, device_id_type=MESH)

    @pl.when(has_north)
    def _():
        pl.semaphore_signal(barrier, inc=1, device_id={"lat": lat + 1}, device_id_type=MESH)

    @pl.when(has_south)
    def _():
        pl.semaphore_signal(barrier, inc=1, device_id={"lat": lat - 1}, device_id_type=MESH)

    @pl.when(is_top)
    def _():
        pl.semaphore_signal(barrier, inc=1, device_id={"lon": partner}, device_id_type=MESH)

    def load(sem, pairs):
        copies = []
        for i, (src, dst) in enumerate(pairs):
            copy = pltpu.make_async_copy(src, dst, load_sems.at[sem, i])
            copy.start()
            copies.append(copy)
        return copies

    def load_tiles(sem, t, begin, end):
        lanes = pl.ds(LANES * t, LANES)
        part = pl.ds(begin, end - begin)
        return load(
            sem,
            [
                (cur_hbm.at[:, :, part, lanes], st.at[t, 0:4, :, part, :]),
                (bef_hbm.at[:, :, part, lanes], st.at[t, 4:8, :, part, :]),
                (tm_hbm.at[:, part, lanes], mk.at[t, 0, :, part, :]),
                (um_hbm.at[:, part, lanes], mk.at[t, 1, :, part, :]),
                (vm_hbm.at[:, part, lanes], mk.at[t, 2, :, part, :]),
            ],
        )

    part = pl.ds(high, SUB)
    highest = load(
        0,
        [
            (cur_hbm.at[:, :, part, :], raw.at[0:4]),
            (bef_hbm.at[:, :, part, :], raw.at[4:8]),
            (tm_hbm.at[:, part, :], raw_flags.at[0]),
            (um_hbm.at[:, part, :], raw_flags.at[1]),
            (vm_hbm.at[:, part, :], raw_flags.at[2]),
        ],
    )
    half = strips // 2
    eastern = [
        load_tiles(1, chunks - 1, 0, SUB * half),
        load_tiles(2, chunks - 1, SUB * half, high),
    ]

    greetings = 3 + has_south.astype(jnp.int32) - answers.astype(jnp.int32)

    lane = lax.broadcasted_iota(jnp.int32, (SUB, LANES), 1)
    first, last = lane == 0, lane == LANES - 1
    nothing = jnp.zeros((SUB, LANES), jnp.float32)

    def masked(t, l, strip, total, x=None, m=None):
        if x is None:
            x = [st[t, f, l, strip, :] for f in range(8)]
            m = [mk[t, i, l, strip, :] for i in range(3)]
        m = [y.astype(jnp.float32) for y in m]
        fm = [m[0], m[0], m[1], m[2]]
        x = [x[f] * fm[f % 4] for f in range(8)]
        for f in range(8):
            st[t, f, l, strip, :] = x[f]
        rho = haline * x[1] - thermal * x[0]
        total = rho if total is None else total + rho
        pr[t, l, strip, :] = total - 0.5 * rho
        return x, m, total

    def strip_of(r):
        return pl.ds(pl.multiple_of(SUB * r, SUB), SUB)

    group = LANES // 4

    def pack(packs, values, c, source):
        packs = list(packs)
        for f, x in values:
            place = group * (f % 4) + c
            moved = pltpu.roll(x, (place - source) & (LANES - 1), 1)
            packs[f // 4] = jnp.where(lane == place, moved, packs[f // 4])
        return packs

    def eastern_strip(r, packs):
        total = None
        for l in range(levels):
            x, m, total = masked(chunks - 1, l, strip_of(r), total)
            packs = pack(packs, enumerate(x + [m[1]]), r * levels + l, LANES - 1)
        return tuple(packs)

    def western_strip(r, packs):
        total = None
        for l in range(levels):
            x, m, total = masked(0, l, strip_of(r), total)
            packs = pack(packs, enumerate(x), r * levels + l, 0)
        return tuple(packs)

    def outer_flags(r, packs):
        strip = strip_of(r)
        packs = list(packs)
        for l in range(levels):
            for i, (t, source) in enumerate(((0, 0), (chunks - 1, LANES - 1))):
                m = [mk[t, j, l, strip, :].astype(jnp.float32) for j in range(3)]
                values = ((0, m[0]), (1, m[0]), (2, m[1]), (3, m[2]))
                packs[i] = pack([packs[i]], values, r * levels + l, source)[0]
        return tuple(packs)

    def middle_strip(strip):
        for t in middle:
            total = None
            for l in range(levels):
                total = masked(t, l, strip, total)[2]

    def edge_row(to, row):
        for t in range(chunks):
            for l in range(levels):
                for f in range(8):
                    at = f * levels + l
                    to[t, at : at + 1, :] = st[t, f, l, row : row + 1, :]
                for f, i in ((8, 2), (9, 0), (10, 1)):
                    mask = mk[t, i, l, row : row + 1, :].astype(jnp.float32)
                    at = f * levels + l
                    to[t, at : at + 1, :] = mask

    def remote(src, dst, which, device):
        return pltpu.make_async_remote_copy(
            src_ref=src,
            dst_ref=dst,
            send_sem=send_sems.at[which],
            recv_sem=recv_sems.at[which],
            device_id=device,
            device_id_type=MESH,
        )

    to_west = remote(own_w, from_e, 0, {"lon": west})
    to_east = remote(own_e, from_w, 1, {"lon": east})
    to_north = remote(top.at[:, 0 : 9 * levels], from_s, 2, {"lat": lat + 1})
    to_south = remote(bottom.at[:, 0 : 8 * levels], from_n, 3, {"lat": lat - 1})
    to_fold = [
        remote(top.at[t, 0 : 8 * levels], from_n.at[t], 4 + t, {"lon": partner}) for t in range(chunks)
    ]

    for copy in highest:
        copy.wait()
    top_strip = slice(high, rows)
    for t in range(chunks):
        lanes = slice(LANES * t, LANES * (t + 1))
        total = None
        for l in range(levels):
            m = [raw_flags[i, l, :, lanes] for i in range(3)]
            for i in range(3):
                mk[t, i, l, top_strip, :] = m[i]
            x = [raw[f, l, :, lanes] for f in range(8)]
            total = masked(t, l, top_strip, total, x, m)[2]
    edge_row(top, rows - 1)

    @pl.when(jnp.logical_and(is_top, sends_first))
    def _():
        pl.semaphore_wait(barrier, greetings)
        for copy in to_fold:
            copy.start()

    packs = [nothing] * 3
    for l in range(levels):
        x = [st[chunks - 1, f, l, top_strip, :] for f in range(8)]
        x.append(mk[chunks - 1, 1, l, top_strip, :].astype(jnp.float32))
        packs = pack(packs, enumerate(x), (strips - 1) * levels + l, LANES - 1)
    packs = tuple(packs)
    for copy in eastern[0]:
        copy.wait()
    packs = lax.fori_loop(0, half, eastern_strip, packs)
    for copy in eastern[1]:
        copy.wait()
    western = load_tiles(3, 0, 0, high)
    inner = [load_tiles(3 + t, t, 0, high) for t in middle]
    packs = lax.fori_loop(half, strips - 1, eastern_strip, packs)
    for f in range(3):
        own_e[f] = packs[f]

    @pl.when(has_north)
    def _():
        pl.semaphore_wait(barrier, greetings)

    @pl.when(sends_first)
    def _():
        to_east.start()

    @pl.when(has_north)
    def _():
        to_north.start()

    packs = [nothing] * 2
    for l in range(levels):
        x = [st[0, f, l, top_strip, :] for f in range(8)]
        packs = pack(packs, enumerate(x), (strips - 1) * levels + l, 0)
    for copy in western:
        copy.wait()
    packs = lax.fori_loop(0, strips - 1, western_strip, tuple(packs))
    for f in range(2):
        own_w[f] = packs[f]
    @pl.when(jnp.logical_and(sends_first, starts))
    def _():
        to_west.start()

    def middle_step(r, carry):
        middle_strip(strip_of(r))
        return carry

    for copies in inner:
        for copy in copies:
            copy.wait()
    lax.fori_loop(0, strips - 1, middle_step, 0)
    edge_row(bottom, 0)

    @pl.when(jnp.logical_and(sends_first, has_south))
    def _():
        to_south.start()

    packs = lax.fori_loop(0, strips, outer_flags, (nothing,) * 2)
    for i in range(2):
        flags[i] = packs[i]

    for t in range(chunks):
        for l in range(levels):
            for f in range(8):
                st[t, f, l, rows : rows + SUB, :] = nothing
            for k in range(4):
                fn[t, k, l, 0:SUB, :] = nothing
            pr[t, l, rows : rows + SUB, :] = nothing

    advect = advect_coef * 0.5 * twice_step
    diffuse = diffuse_coef * twice_step
    push = gravity * twice_step
    keep = 1.0 - 2.0 * asselin

    def step_strip(r, carry):
        at = pl.multiple_of(SUB * r, SUB)
        strip, above = pl.ds(at, SUB), pl.ds(at + 1, SUB)
        put, below = pl.ds(at + SUB, SUB), pl.ds(at + SUB - 1, SUB)
        row = lat * rows + r * SUB + lax.broadcasted_iota(jnp.int32, (SUB, LANES), 0)
        cor = coriolis * (2.0 * (row.astype(jnp.float32) + 0.5) / (rows * n_lat) - 1.0)
        cor = twice_step * cor

        def finish(l, t, west_flux, east_flux):
            lanes = pl.ds(LANES * t, LANES)
            h = [st[t, f, l, strip, :] for f in range(8)]
            n = [st[t, f, l, above, :] for f in range(8)]
            m = [mk[t, i, l, strip, :].astype(jnp.float32) for i in range(3)]
            fm = [m[0], m[0], m[1], m[2]]
            p = pr[t, l, strip, :]
            speed, mask = advect * h[3], diffuse * m[2]
            tend = []
            for k in range(4):
                flux_n = speed * (h[k] + n[k]) - mask * (n[4 + k] - h[4 + k])
                fn[t, k, l, put, :] = flux_n
                tend.append((west_flux[k] - east_flux[k]) + (fn[t, k, l, below, :] - flux_n))
            tend[2] = tend[2] + (cor * h[3] + push * m[1] * p)
            tend[3] = tend[3] - (cor * h[2] + push * m[2] * (pr[t, l, above, :] - p))
            for k in range(4):
                after = (h[4 + k] + tend[k]) * fm[k]
                after_ref[k, l, strip, lanes] = after
                filt_ref[k, l, strip, lanes] = keep * h[k] + asselin * (h[4 + k] + after)

        for l in range(levels):
            prior_speed = jnp.full((SUB, LANES), DRY, jnp.float32)
            prior_part = [nothing] * 4
            waiting = None
            for t in range(chunks):
                h = [st[t, f, l, strip, :] for f in range(8)]
                wet = mk[t, 1, l, strip, :]
                speed, mask = advect * h[2], diffuse * wet.astype(jnp.float32)
                moved = pltpu.roll(jnp.where(wet > 0, h[2], DRY), 1, 1)
                speed_w = jnp.where(first, prior_speed, moved)
                prior_speed = moved
                dry = speed_w > 0.5 * DRY
                speed_w = jnp.where(dry, 0.0, advect * speed_w)
                mask_w = jnp.where(dry, 0.0, diffuse)
                flux_w, back = [], []
                for k in range(4):
                    part = pltpu.roll(speed * h[k] + mask * h[4 + k], 1, 1)
                    flux = jnp.where(first, prior_part[k], part)
                    prior_part[k] = part
                    flux = flux + (speed_w * h[k] - mask_w * h[4 + k])
                    if t == 0:
                        flux = jnp.where(first, 0.0, flux)
                    flux_w.append(flux)
                    carried = flux
                    if k == 2:
                        carried = flux + (push / diffuse) * mask_w * pr[t, l, strip, :]
                    back.append(pltpu.roll(carried, LANES - 1, 1))
                if waiting is not None:
                    flux_e = [jnp.where(last, y, x) for x, y in zip(waiting[1], back)]
                    finish(l, t - 1, waiting[0], flux_e)
                waiting = flux_w, back
            flux_e = [jnp.where(last, 0.0, x) for x in waiting[1]]
            finish(l, chunks - 1, waiting[0], flux_e)
        return carry

    lax.fori_loop(0, strips, step_strip, 0)

    @pl.when(sends_last)
    def _():
        pl.semaphore_wait(barrier, greetings)
        for copy in to_fold:
            copy.start()
        to_south.start()
        to_east.start()

    @pl.when(jnp.logical_and(sends_last, starts))
    def _():
        to_west.start()

    def field(ref, t, f):
        return ref[t, f * levels : (f + 1) * levels, :]

    @pl.when(has_south)
    def _():
        to_north.wait_recv()
        for t in range(chunks):
            h = [field(from_s, t, f) for f in range(9)]
            a = [field(bottom, t, f) for f in range(11)]
            fm = [a[9], a[9], a[10], a[8]]
            speed, mask = advect * h[3], diffuse * h[8]
            for k in range(4):
                flux = speed * (h[k] + a[k]) - mask * (a[4 + k] - h[4 + k])
                south_ref[t, k] = flux * fm[k]

    @pl.when(lat == 0)
    def _():
        south_ref[...] = jnp.zeros(south_ref.shape, jnp.float32)

    to_east.wait_recv()

    @pl.when(answers)
    def _():
        to_west.start()

    to_west.wait_recv()

    def spread(x, g):
        x = jnp.where(lane // group == g, x, 0.0)
        x = x + pltpu.roll(x, group, 1)
        return x + pltpu.roll(x, 2 * group, 1)

    def outer_flux(left, right):
        speed, mask = spread(left[0], 2), spread(left[2], 0)
        flux = advect * speed * (left[0] + right[0]) - diffuse * mask * (right[1] - left[1])
        return flux, mask

    flux_w, _ = outer_flux(from_w, own_w)
    flux_e, mask = outer_flux(own_e, from_e)
    rho = haline * pltpu.roll(from_e[0], LANES - group, 1) - thermal * from_e[0]
    pres = 0.5 * rho
    level = lane % levels
    for l in range(1, levels):
        pres = pres + jnp.where(level >= l, pltpu.roll(rho, l, 1), 0.0)
    pres = jnp.where(lane // group == 2, pltpu.roll(pres, 2 * group, 1), 0.0)
    flux_w = flux_w * flags[0]
    flux_e = -(flux_e + push * mask * pres) * flags[1]
    even = (lane & 1) == 0
    pair = ((lane + 1) // 2) & (LANES // 2 - 1)
    for k in range(4):
        index = (pair + group * k) & (LANES - 1)
        one, other = (
            jnp.take_along_axis(x, index, axis=1, mode="promise_in_bounds")
            for x in (flux_w, flux_e)
        )
        outer_ref[k] = jnp.where(even, one, other)

    @pl.when(has_north)
    def _():
        to_south.wait_recv()

    @pl.when(is_top)
    def _():
        for copy in to_fold:
            copy.wait_recv()
        shape = from_n.shape[1:]
        mirror = LANES - 1 - lax.broadcasted_iota(jnp.int32, shape, 1)
        scalar = lax.broadcasted_iota(jnp.int32, shape, 0) // levels % 4 < 2

        def turned(x):
            x = jnp.take_along_axis(x, mirror, axis=1, mode="promise_in_bounds")
            return jnp.where(scalar, x, -x)

        for t in range((chunks + 1) // 2):
            a, b = from_n[t], from_n[chunks - 1 - t]
            from_n[t] = turned(b)
            from_n[chunks - 1 - t] = turned(a)

    for t in range(chunks):
        h = [field(top, t, f) for f in range(11)]
        a = [field(from_n, t, f) for f in range(8)]
        fm = [h[9], h[9], h[10], h[8]]
        speed, mask = advect * h[3], diffuse * h[8]
        rho = haline * a[1] - thermal * a[0]
        total, pres = None, []
        for l in range(levels):
            one = rho[l : l + 1, :]
            total = one if total is None else total + one
            pres.append(total - 0.5 * one)
        for k in range(4):
            change = mask * a[4 + k] - speed * a[k]
            if k == 3:
                change = change - push * h[8] * jnp.concatenate(pres, 0)
            north_ref[t, k] = change * fm[k]

    to_west.wait_send()
    to_east.wait_send()

    @pl.when(has_north)
    def _():
        to_north.wait_send()

    @pl.when(has_south)
    def _():
        to_south.wait_send()

    @pl.when(is_top)
    def _():
        for copy in to_fold:
            copy.wait_send()


def closing_kernel(
    after_ref,
    filt_ref,
    outer_ref,
    south_ref,
    north_ref,
    after_hbm,
    filt_hbm,
    edge,
    ribbon,
    sems,
):
    _, levels, rows, cols = after_ref.shape
    chunks = cols // LANES
    strips = rows // SUB
    blocks, targets = (after_ref, filt_ref), (after_hbm, filt_hbm)
    copies = []

    def store(src, dst):
        copy = pltpu.make_async_copy(src, dst, sems.at[len(copies)])
        copy.start()
        copies.append(copy)

    inner_lanes = pl.ds(LANES, cols - 2 * LANES)
    inner_rows = pl.ds(SUB, rows - 2 * SUB)
    for src, dst in zip(blocks, targets):
        place = (slice(None), slice(None), inner_rows, inner_lanes)
        store(src.at[place], dst.at[place])

    lane = lax.broadcasted_iota(jnp.int32, (SUB, LANES), 1)
    sub = lax.broadcasted_iota(jnp.int32, (SUB, LANES), 0)
    sides = ((south_ref, 0, 0), (north_ref, rows - SUB, SUB - 1))

    def row_change(ref, t, k, l, where):
        one = jnp.broadcast_to(ref[t, k, l : l + 1, :], (SUB, LANES))
        return jnp.where(sub == where, one, 0.0)

    for i, (ref, row, where) in enumerate(sides):
        for k in range(4):
            for l in range(levels):
                for t in range(1, chunks - 1):
                    lanes = pl.ds(LANES * t, LANES)
                    change = row_change(ref, t, k, l, where)
                    to = pl.ds(LANES * (t - 1), LANES)
                    ribbon[0, i, k, l, :, to] = after_ref[k, l, row : row + SUB, lanes] + change
                    ribbon[1, i, k, l, :, to] = (
                        filt_ref[k, l, row : row + SUB, lanes] + asselin * change
                    )
        for o in range(2):
            store(ribbon.at[o, i], targets[o].at[:, :, pl.ds(row, SUB), inner_lanes])

    def outer_strip(r, carry):
        strip = pl.ds(pl.multiple_of(SUB * r, SUB), SUB)
        for k in range(4):
            for l in range(levels):
                one = pltpu.roll(outer_ref[k], LANES - 2 * (r * levels + l), 1)
                for i, (t, where) in enumerate(((0, 0), (chunks - 1, LANES - 1))):
                    lanes = pl.ds(LANES * t, LANES)
                    change = jnp.where(lane == where, one, 0.0)
                    edge[0, i, k, l, strip, :] = after_ref[k, l, strip, lanes] + change
                    edge[1, i, k, l, strip, :] = filt_ref[k, l, strip, lanes] + asselin * change
        return carry

    piece = rows // PIECES
    for part in range(PIECES):
        lax.fori_loop(part * piece // SUB, (part + 1) * piece // SUB, outer_strip, 0)
        for ref, row, where in sides:
            if part * piece <= row < (part + 1) * piece:
                for k in range(4):
                    for l in range(levels):
                        for i, t in enumerate((0, chunks - 1)):
                            change = row_change(ref, t, k, l, where)
                            edge[0, i, k, l, row : row + SUB, :] += change
                            edge[1, i, k, l, row : row + SUB, :] += asselin * change
        span = pl.ds(part * piece, piece)
        for o in range(2):
            for i, t in enumerate((0, chunks - 1)):
                store(
                    edge.at[o, i, :, :, span, :],
                    targets[o].at[:, :, span, pl.ds(LANES * t, LANES)],
                )

    for copy in copies:
        copy.wait()


def shards(n_lon, n_lat, *args):
    _, levels, rows, cols = args[0].shape
    chunks = cols // LANES
    f32 = jnp.float32
    out = jax.ShapeDtypeStruct(args[0].shape, f32)
    args = [pltpu.with_memory_space_constraint(x, pltpu.HBM) for x in args]
    block = pl.BlockSpec(memory_space=pltpu.VMEM)
    parts = pl.pallas_call(
        functools.partial(kernel, n_lon, n_lat),
        out_shape=(
            out,
            out,
            jax.ShapeDtypeStruct((4, SUB, LANES), f32),
            jax.ShapeDtypeStruct((chunks, 4, levels, LANES), f32),
            jax.ShapeDtypeStruct((chunks, 4, levels, LANES), f32),
        ),
        in_specs=[pl.BlockSpec(memory_space=pl.ANY)] * 5,
        out_specs=(block,) * 5,
        scratch_shapes=[
            pltpu.VMEM((chunks, 8, levels, rows + SUB, LANES), f32),
            pltpu.VMEM((chunks, 3, levels, rows, LANES), jnp.int32),
            pltpu.VMEM((chunks, levels, rows + SUB, LANES), f32),
            pltpu.VMEM((chunks, 4, levels, rows + SUB, LANES), f32),
            pltpu.VMEM((8, levels, SUB, cols), f32),
            pltpu.VMEM((3, levels, SUB, cols), jnp.int32),
            pltpu.VMEM((3, SUB, LANES), f32),
            pltpu.VMEM((2, SUB, LANES), f32),
            pltpu.VMEM((2, SUB, LANES), f32),
            pltpu.VMEM((2, SUB, LANES), f32),
            pltpu.VMEM((3, SUB, LANES), f32),
            pltpu.VMEM((chunks, 11 * levels, LANES), f32),
            pltpu.VMEM((chunks, 11 * levels, LANES), f32),
            pltpu.VMEM((chunks, 8 * levels, LANES), f32),
            pltpu.VMEM((chunks, 9 * levels, LANES), f32),
            pltpu.SemaphoreType.DMA((chunks + 2, 5)),
            pltpu.SemaphoreType.DMA((4 + chunks,)),
            pltpu.SemaphoreType.DMA((4 + chunks,)),
        ],
        compiler_params=pltpu.CompilerParams(
            collective_id=0, has_side_effects=True, vmem_limit_bytes=28 << 20
        ),
    )(*args)
    parts = [pltpu.with_memory_space_constraint(x, pltpu.VMEM) for x in parts]
    return pl.pallas_call(
        closing_kernel,
        out_shape=(out, out),
        in_specs=[block] * 5,
        out_specs=(pl.BlockSpec(memory_space=pl.ANY),) * 2,
        scratch_shapes=[
            pltpu.VMEM((2, 2, 4, levels, rows, LANES), f32),
            pltpu.VMEM((2, 2, 4, levels, SUB, cols - 2 * LANES), f32),
            pltpu.SemaphoreType.DMA((6 + 4 * PIECES,)),
        ],
        compiler_params=pltpu.CompilerParams(vmem_limit_bytes=28 << 20),
    )(*parts)


def solution(mesh):
    state = P(None, None, "lat", "lon")
    flags = P(None, "lat", "lon")
    return jax.shard_map(
        functools.partial(shards, mesh.shape["lon"], mesh.shape["lat"]),
        mesh=mesh,
        in_specs=(state, state, flags, flags, flags),
        out_specs=(state, state),
        check_vma=False,
    )
```
